512 devices in a mesh: space: 128 (over y, z, core), chan: 4 (over x).
Axes of the slice: x: 4, y: 4, z: 16, core: 2. Of those that a mesh axis runs over, the one named last changes fastest.
Arguments:
- features: bfloat16 [512, 128, 512], P('space', 'chan'), may hold values from -6 to 6
- occupancy: int32 [512, 512], P('space'), may hold values 0 or 1
- weight: bfloat16 [256, 27, 128], P('chan'), may hold values from -0.109375 to 0.109375
- cotangent: bfloat16 [512, 256, 512], P('space', 'chan'), may hold values from -6 to 6
- neighbours: int32 [512, 26], P('space'), may hold values from -1 to 511, as said below
Outputs:
- activation: bfloat16 [512, 256, 512], P('space', 'chan')
- input_grad: bfloat16 [512, 128, 512], P('space', 'chan')
- weight_grad: float32 [256, 27, 128], P('chan')
The draws below stay inside these ranges and needn't reach their ends.
Inputs may be any that keep to these rules, and one draw needn't show every extreme that they name: `neighbours`: each entry is -1 or a block id. With o = id // 4 the listing block's owner, an entry names a block of owner o, or, only for a listing block among the first 1 of its owner and only in columns 0 to 12, one of the last 1 block of owner o - 1, or, only for a listing block among the last 1 of its owner and only in columns 13 to 25, one of the first 1 block of owner o + 1. The same block may appear in several directions.
All inputs are finite; a program needn't handle non-finite values. No bound on the sum of `occupancy` on one device may be relied on, other than what follows from the above.
Results may differ from the reference program's by a relative error of at most 0.0049.
Values may be sent and summed in bfloat16 or wider, within the bound.
No kernel may reach another device: no remote copies, remote signals or barrier semaphores. Data moves between devices by JAX's collectives and lax.ppermute only.
A program may use at most 64 MiB of HBM per device.

```python
import jax
import jax.numpy as jnp
from jax import lax

CIN = 128
COUT = 256
B_DEV = 4
BLOCKS = 512


def draw_neighbours(key, part):
    key = jax.random.fold_in(key, 11)
    first, second, third, fourth = jax.random.split(key, 4)
    rim_count = B_DEV // 4
    ids = jnp.arange(BLOCKS, dtype=jnp.int32)
    home = ids // B_DEV
    local_index = ids % B_DEV
    column = jnp.arange(26, dtype=jnp.int32)[None, :]
    lower_side = (local_index[:, None] < rim_count) & (column < 13)
    upper_side = (local_index[:, None] >= B_DEV - rim_count) & (column >= 13)
    boundary_passing = jax.random.randint(first, (BLOCKS, 26), 0, 2) == 1
    inside = home[:, None] * B_DEV + jax.random.randint(second, (BLOCKS, 26), 0, B_DEV)
    rim_pick = jax.random.randint(third, (BLOCKS, 26), 0, rim_count)
    below = (home[:, None] - 1) * B_DEV + B_DEV - 1 - rim_pick
    above = (home[:, None] + 1) * B_DEV + rim_pick
    result = jnp.where(lower_side & boundary_passing, below, jnp.where(upper_side & boundary_passing, above, inside))
    outside = (result < 0) | (result >= BLOCKS)
    empty = (jax.random.randint(fourth, (BLOCKS, 26), 0, 4) == 0) | outside
    result = jnp.where(empty, -1, result)
    result = result.at[0, 0].set(-1).at[BLOCKS - 1, 25].set(BLOCKS - 1)
    result = result.at[B_DEV, 0].set(B_DEV - 1).at[B_DEV - 1, 25].set(B_DEV)
    return result.astype(jnp.int32)


def with_ends(values, stream_key, smallest, top_value):
    longest = values.shape.index(max(values.shape))
    spots = []
    for shift in (0, 1):
        where = [jax.random.randint(jax.random.fold_in(stream_key, axis), (), 0, length) for axis, length in enumerate(values.shape)]
        where[longest] = (where[longest] + shift) % values.shape[longest]
        spots.append(tuple(where))
    return values.at[spots[0]].set(smallest).at[spots[1]].set(top_value)


def block_scale(rng, shape, cuts, low, high):
    level = 1.0
    for dim, shards_of in cuts:
        steps = jax.random.uniform(jax.random.fold_in(jax.random.fold_in(rng, 6), dim), (shards_of,), jnp.float32, low / len(cuts), high / len(cuts))
        level = level * jnp.repeat(jnp.exp(steps), shape[dim] // shards_of).reshape((-1,) + (1,) * (len(shape) - 1 - dim))
    return level


def scatter_about(key, extent, scale, limit, cuts=(), kind=jnp.bfloat16):
    drawn = jax.random.normal(key, extent, jnp.float32) * scale
    if len(cuts) > 0:
        drawn = block_scale(key, extent, cuts, -0.22, 0.18) * drawn
    return jnp.clip(drawn, min=-limit, max=limit).astype(kind)


def setup_inputs(seed: int = 0) -> dict:
    key_of = jax.random.split(jax.random.key(seed), 6)
    return {
        "features": scatter_about(key_of[0], (BLOCKS, CIN, 512), 1.0, 6.0, ((0, 128), (1, 4))),
        "occupancy": with_ends((jax.random.randint(key_of[1], (BLOCKS, 512), 0, 2) < 1).astype(jnp.int32), jax.random.fold_in(key_of[1], 1), 0, 1),
        "weight": scatter_about(key_of[2], (COUT, 27, CIN), (27 * CIN) ** -0.5, 0.109375, ((0, 4),)),
        "cotangent": scatter_about(key_of[3], (BLOCKS, COUT, 512), 1.0, 6.0, ((0, 128), (1, 4))),
        "neighbours": draw_neighbours(jax.random.fold_in(key_of[5], 71), 0),
    }


def offset_list():
    return [(a, b, c) for a in (-1, 0, 1) for b in (-1, 0, 1) for c in (-1, 0, 1)]

def span_pair(shift):
    if shift < 0:
        return ((0, 1), (7, 8))
    if shift == 0:
        return ((1, 9), (0, 8))
    return ((9, 10), (0, 1))

def cuts_for(a, b, c):
    spans = [span_pair(shift) for shift in (a, b, c)]
    padding_trimmed = (slice(None),) + tuple((slice(pair[0][0], pair[0][1]) for pair in spans))
    block_cut = (slice(None),) + tuple((slice(pair[1][0], pair[1][1]) for pair in spans))
    return (padding_trimmed, block_cut)

def assemble(blocks):
    channels = blocks.shape[1]
    cube_view = blocks.reshape(27, channels, 8, 8, 8)
    padded = jnp.zeros((channels, 10, 10, 10), blocks.dtype)
    for position, (a, b, c) in enumerate(offset_list()):
        padding_trimmed, block_cut = cuts_for(a, b, c)
        padded = padded.at[padding_trimmed].set(cube_view[position][block_cut])
    return padded

def cut_patch(padded, a, b, c):
    return padded[:, 1 + a:9 + a, 1 + b:9 + b, 1 + c:9 + c].reshape(padded.shape[0], 512)

def unpatch(grads):
    channels = grads[0].shape[0]
    padded_grad = jnp.zeros((channels, 10, 10, 10), jnp.float32)
    for position, (a, b, c) in enumerate(offset_list()):
        padded_grad = padded_grad.at[:, 1 + a:9 + a, 1 + b:9 + b, 1 + c:9 + c].add(grads[position].reshape(channels, 8, 8, 8))
    return padded_grad

def spread(padded_grad):
    channels = padded_grad.shape[0]
    pieces = []
    for a, b, c in offset_list():
        padding_trimmed, block_cut = cuts_for(a, b, c)
        piece_grid = jnp.zeros((channels, 8, 8, 8), jnp.float32).at[block_cut].set(padded_grad[padding_trimmed])
        pieces.append(piece_grid.reshape(channels, 512))
    return jnp.stack(pieces)

def reference(features, occupancy, weight, cotangent, neighbours):
    active_voxel_mask = occupancy.astype(jnp.bfloat16)
    mask_applied = features * active_voxel_mask[:, None, :]
    blocks_total = features.shape[0]
    self_ids = jnp.arange(blocks_total, dtype=jnp.int32)[:, None]
    every_index_list = jnp.concatenate([neighbours[:, :13], self_ids, neighbours[:, 13:]], axis=1).astype(jnp.int32)
    weight32 = weight.astype(jnp.float32)
    cout = weight.shape[0]
    cin = weight.shape[2]

    def visit(totals, position):
        weight_running_sum, grad_acc = totals
        row_ids = every_index_list[position]
        present = row_ids >= 0
        safe_ids = jnp.maximum(row_ids, 0)
        blocks = mask_applied[safe_ids] * present.astype(jnp.bfloat16)[:, None, None]
        padded = assemble(blocks)
        patches = jnp.stack([cut_patch(padded, a, b, c) for a, b, c in offset_list()]).astype(jnp.float32)
        pre_act = jnp.einsum('okc,kcv->ov', weight32, patches)
        live_row = occupancy[position].astype(jnp.float32)[None, :]
        output = (jax.nn.silu(pre_act) * live_row).astype(jnp.bfloat16)
        sigma = jax.nn.sigmoid(pre_act)
        slope = sigma * (1.0 + pre_act * (1.0 - sigma))
        grad_pre = (cotangent[position].astype(jnp.float32) * slope * live_row).astype(jnp.bfloat16)
        grad_pre32 = grad_pre.astype(jnp.float32)
        weight_running_sum = weight_running_sum + jnp.einsum('ov,kcv->okc', grad_pre32, patches)
        grad_patches = jnp.einsum('okc,ov->kcv', weight32, grad_pre32)
        pieces = spread(unpatch(grad_patches)) * present.astype(jnp.float32)[:, None, None]
        grad_acc = grad_acc.at[safe_ids].add(pieces)
        return ((weight_running_sum, grad_acc), output)
    start = (jnp.zeros((cout, 27, cin), jnp.float32), jnp.zeros((blocks_total, cin, 512), jnp.float32))
    (weight_running_sum, grad_acc), activation = lax.scan(visit, start, jnp.arange(blocks_total, dtype=jnp.int32))
    input_grad = (grad_acc * occupancy.astype(jnp.float32)[:, None, :]).astype(jnp.bfloat16)
    weight_grad = weight_running_sum * lax.rsqrt(jnp.float32(blocks_total * 512))
    return (activation, input_grad, weight_grad)
```

```python
import functools

import jax
import jax.numpy as jnp
from jax import lax
from jax.experimental import pallas as pl
from jax.experimental.pallas import tpu as pltpu
from jax.sharding import PartitionSpec as P

F32 = jnp.float32
BF16 = jnp.bfloat16
OFFSETS = [(a, b, c) for a in (-1, 0, 1) for b in (-1, 0, 1) for c in (-1, 0, 1)]
NT = (((1,), (1,)), ((), ()))
CUBE = 1616
WIDE = 640
VMEM = pl.BlockSpec(memory_space=pltpu.VMEM)
SMEM = pl.BlockSpec(memory_space=pltpu.SMEM)
PARAMS = pltpu.CompilerParams(vmem_limit_bytes=48 * 1024 * 1024)


def spans(shift):
    if shift < 0:
        return [(0, 7)]
    if shift > 0:
        return [(9, 0)]
    return [(1 + i, i) for i in range(8)]


def fill_cube(slots, block, voxels, cube, base):
    for number, (a, b, c) in enumerate(OFFSETS):
        first = pl.multiple_of(slots[block, number] * 512, 512)
        for i_to, i_from in spans(a):
            if c == 0:
                for j_to, j_from in spans(b):
                    row = base + (i_to * 10 + j_to) * 16 + 8
                    cube[row : row + 8, :] = voxels[pl.ds(first + i_from * 64 + j_from * 8, 8), :]
                continue
            k_from, k_to = (7, 7) if c < 0 else (0, 16)
            if b == 0:
                source = pl.ds(first + i_from * 64 + k_from, 8, stride=8)
                cube[pl.ds(base + (i_to * 10 + 1) * 16 + k_to, 8, stride=16), :] = voxels[source, :]
            else:
                ((j_to, j_from),) = spans(b)
                row = base + (i_to * 10 + j_to) * 16 + k_to
                source = pl.ds(first + i_from * 64 + j_from * 8 + k_from, 1)
                cube[row : row + 1, :] = voxels[source, :]


def pack_patches(cube, base, patches, top):
    for i in range(10):
        for c in range(3):
            rows = [
                cube[base + (i * 10 + j) * 16 + 7 + c : base + (i * 10 + j) * 16 + 15 + c, :]
                for j in range(10)
            ]
            pairs = [
                jnp.concatenate([rows[j], rows[j + 1]], axis=0).astype(BF16) for j in range(9)
            ]
            for b in range(3):
                lanes = (3 * b + c) * 128
                for t in range(4):
                    row = top + i * 64 + t * 16
                    patches[row : row + 16, lanes : lanes + 128] = pairs[2 * t + b]


def stack_weight(weight, stacked):
    out = weight.shape[1]
    for number in range(27):
        a, lanes = number // 9, number % 9 * 128
        stacked[a * out : (a + 1) * out, lanes : lanes + 128] = weight[number]


def forward_kernel(
    blocks, slots, gathered, weight, cotangent, occupancy,
    activation, stacked, grads, tiles,
    voxels, cube, patches,
):
    stack_weight(weight, stacked)
    for slot in range(blocks + 2):
        block = jnp.concatenate([gathered[c, slot] for c in range(gathered.shape[0])], axis=0)
        voxels[slot * 512 : (slot + 1) * 512, :] = block.astype(F32).T
    voxels[(blocks + 2) * 512 : (blocks + 3) * 512, :] = jnp.zeros((512, 128), F32)
    for p in range(blocks):
        fill_cube(slots, p, voxels, cube, p * CUBE)
        pack_patches(cube, p * CUBE, patches, p * WIDE)
        wide = lax.dot_general(
            stacked[...], patches[p * WIDE : (p + 1) * WIDE, :], NT, preferred_element_type=F32
        )
        pre = (
            wide[0:64, 0:512]
            + pltpu.roll(wide[64:128], WIDE - 64, 1)[:, 0:512]
            + wide[128:192, 128:640]
        )
        live = occupancy[p : p + 1, :].astype(F32)
        sigma = jax.nn.sigmoid(pre)
        activation[p] = (pre * sigma * live).astype(BF16)
        slope = sigma * (1.0 + pre * (1.0 - sigma))
        grad = (cotangent[p].astype(F32) * slope * live).astype(BF16).astype(F32)
        grad = jnp.concatenate([grad, jnp.zeros((64, 128), F32)], axis=1)
        lanes = slice(p * WIDE, (p + 1) * WIDE)
        grads[0:64, lanes] = grad.astype(BF16)
        grads[64:128, lanes] = pltpu.roll(grad, 64, 1).astype(BF16)
        grads[128:192, lanes] = pltpu.roll(grad, 128, 1).astype(BF16)
    for first in range(0, 9, 2):
        count = min(2, 9 - first)
        part = jnp.dot(
            grads[...],
            patches[:, first * 128 : (first + count) * 128],
            preferred_element_type=F32,
        )
        for t in range(count):
            for r in range(12):
                corner = part[r * 16 : (r + 1) * 16, t * 128 : (t + 1) * 128]
                tiles[(r // 4 * 9 + first + t) * 4 + r % 4] = corner.astype(BF16)
    for t in range(108, 128):
        tiles[t] = jnp.zeros((16, 128), BF16)


def backward_kernel(
    blocks, slots, stacked, grads, own, rims, sums, wide
):
    sums[...] = jnp.zeros_like(sums)
    row_index = lax.broadcasted_iota(jnp.int32, (64, 128), 0) % 8
    edge = lax.broadcasted_iota(jnp.int32, (8, 128), 0)
    for p in range(blocks):
        turn = grads[:, p * WIDE : (p + 1) * WIDE].astype(F32).T.astype(BF16)
        wide[...] = jnp.dot(turn, stacked[...], preferred_element_type=F32)
        for i in range(10):
            a, i_to = (-1, 7) if i == 0 else ((1, 0) if i == 9 else (0, i - 1))

            def line(j, c):
                total = None
                for b in range(3):
                    if 0 <= j - b < 8:
                        row = i * 64 + (j - b) * 8
                        lanes = (3 * b + c) * 128
                        term = wide[row : row + 8, lanes : lanes + 128]
                        total = term if total is None else total + term
                return total

            for b, js in ((-1, [0]), (0, list(range(1, 9))), (1, [9])):
                before = [pltpu.roll(line(j, 0), 7, 0) for j in js]
                centre = [line(j, 1) for j in js]
                after = [pltpu.roll(line(j, 2), 1, 0) for j in js]
                j_to = 7 if b < 0 else 0
                for c in (-1, 0, 1):
                    if c < 0:
                        parts = [jnp.where(edge == 7, x, 0.0) for x in before]
                    elif c > 0:
                        parts = [jnp.where(edge == 0, x, 0.0) for x in after]
                    else:
                        parts = [
                            y + jnp.where(edge < 7, x, 0.0) + jnp.where(edge > 0, z, 0.0)
                            for x, y, z in zip(before, centre, after)
                        ]
                    part = parts[0] if len(parts) == 1 else jnp.concatenate(parts, axis=0)
                    number = 9 * (a + 1) + 3 * (b + 1) + c + 1
                    first = pl.multiple_of(slots[p, number] * 512, 512)
                    rows = pl.ds(first + i_to * 64 + j_to * 8, 8 * len(js))
                    sums[rows, :] = sums[rows, :] + part
    share = own.shape[2]
    for slot in range(blocks):
        turned = sums[slot * 512 : (slot + 1) * 512, :].T
        for c in range(own.shape[0]):
            own[c, slot] = turned[c * share : (c + 1) * share, :]
    for rim in range(2):
        slot = blocks + rim
        turned = sums[slot * 512 : (slot + 1) * 512, :].T.astype(BF16)
        for c in range(own.shape[0]):
            rims[rim, c] = turned[c * share : (c + 1) * share, :]


def shape(*dims, dtype=BF16):
    return jax.ShapeDtypeStruct(dims, dtype)


def call_forward(slots, gathered, weight, cotangent, occupancy):
    blocks, out = cotangent.shape[:2]
    return pl.pallas_call(
        functools.partial(forward_kernel, blocks),
        out_shape=[
            shape(blocks, out, 512),
            shape(3 * out, 1152),
            shape(3 * out, blocks * WIDE),
            shape(128, 16, 128),
        ],
        in_specs=[SMEM] + [VMEM] * 4,
        out_specs=[VMEM] * 4,
        scratch_shapes=[
            pltpu.VMEM(((blocks + 3) * 512, 128), F32),
            pltpu.VMEM((blocks * CUBE, 128), F32),
            pltpu.VMEM((blocks * WIDE, 1152), BF16),
        ],
        compiler_params=PARAMS,
    )(slots, gathered, weight, cotangent, occupancy)


def call_backward(slots, stacked, grads, chan):
    blocks = slots.shape[0]
    share = 128 // chan
    return pl.pallas_call(
        functools.partial(backward_kernel, blocks),
        out_shape=[shape(chan, blocks, share, 512, dtype=F32), shape(2, chan, share, 512)],
        in_specs=[SMEM, VMEM, VMEM],
        out_specs=[VMEM] * 2,
        scratch_shapes=[
            pltpu.VMEM(((blocks + 3) * 512, 128), F32),
            pltpu.VMEM((WIDE, 1152), F32),
        ],
        compiler_params=PARAMS,
    )(slots, stacked, grads)


def add_kernel(copies, pieces, out):
    total = pieces[0].astype(F32)
    for n in range(1, pieces.shape[0]):
        total = total + pieces[n].astype(F32)
    for n in range(copies):
        out[n] = total.astype(BF16)


def call_add(pieces, copies):
    return pl.pallas_call(
        functools.partial(add_kernel, copies),
        out_shape=shape(copies, *pieces.shape[1:]),
        in_specs=[VMEM],
        out_specs=VMEM,
        compiler_params=PARAMS,
    )(pieces)


def stages_of(count):
    return {128: (4, 16, 2), 4: (2, 1, 2), 8: (2, 2, 2), 16: (2, 4, 2)}[count]


def exchange(pieces, groups):
    return lax.all_to_all(pieces, "space", 0, 0, axis_index_groups=groups)


def on_device(features, occupancy, weight, cotangent, neighbours):
    blocks = features.shape[0]
    out = weight.shape[0]
    space = lax.axis_size("space")
    chan = lax.axis_size("chan")
    columns, rows, cores = stages_of(space)
    place = lax.axis_index("space")
    even = place % 2 == 0

    partner = [(i, i ^ 1) for i in range(space)]
    across = [(i, i - 1 if i % 2 == 0 else i + 1) for i in range(1, space - 1)]
    masked = features * occupancy.astype(BF16)[:, None, :]
    first, last = masked[0], masked[blocks - 1]
    from_partner = lax.ppermute(jnp.where(even, last, first), "space", partner)
    from_across = lax.ppermute(jnp.where(even, first, last), "space", across)
    held = jnp.concatenate([masked, from_partner[None], from_across[None]])
    gathered = lax.all_gather(held, "chan", axis=0)

    ids = jnp.concatenate(
        [
            neighbours[:, :13],
            (place * blocks + jnp.arange(blocks, dtype=jnp.int32))[:, None],
            neighbours[:, 13:],
        ],
        axis=1,
    )
    slots = ids - place * blocks
    below = jnp.where(even, blocks + 1, blocks)
    above = jnp.where(even, blocks, blocks + 1)
    slots = jnp.where(slots == -1, below, jnp.where(slots == blocks, above, slots))
    slots = jnp.where(ids < 0, blocks + 2, slots)

    activation, stacked, grads, tiles = call_forward(
        slots, gathered, jnp.transpose(weight, (1, 0, 2)), cotangent, occupancy
    )

    own, rims = call_backward(slots, stacked, grads, chan)
    to_partner = lax.ppermute(rims[0], "space", partner).astype(F32)
    to_across = lax.ppermute(rims[1], "space", across).astype(F32)
    first = jnp.where(even, to_across, to_partner)
    last = jnp.where(even, to_partner, to_across)
    middle = jnp.zeros((chan, blocks - 2) + first.shape[1:], F32)
    own = own + jnp.concatenate([first[:, None], middle, last[:, None]], axis=1)
    own, tiles = lax.optimization_barrier((own, tiles))
    reduced = lax.psum_scatter(own, "chan", scatter_dimension=0)
    input_grad = (reduced * occupancy.astype(F32)[:, None, :]).astype(BF16)

    near = [
        [(y * rows + z) * cores + c for y in range(columns) for c in range(cores)]
        for z in range(rows)
    ]
    far = [
        [(y * rows + z) * cores + c for z in range(rows)]
        for y in range(columns)
        for c in range(cores)
    ]
    parts = exchange(tiles.reshape(columns * cores, -1, 16, 128), near)
    parts = exchange(call_add(parts, 1).reshape(rows, -1, 16, 128), far)
    total = exchange(call_add(parts, rows), far).reshape(-1, 16, 128)
    total = exchange(jnp.broadcast_to(total, (columns * cores,) + total.shape), near)
    total = total.reshape(128, 16, 128)[:108].astype(F32).reshape(27, out, 128)
    weight_grad = jnp.transpose(total * lax.rsqrt(F32(space * blocks * 512)), (1, 0, 2))
    return (activation, input_grad, weight_grad)


def solution(mesh):
    placed = (
        P("space", "chan", None),
        P("space", None),
        P("chan", None, None),
        P("space", "chan", None),
        P("space", None),
    )
    return jax.shard_map(
        on_device,
        mesh=mesh,
        in_specs=placed,
        out_specs=(P("space", "chan", None), P("space", "chan", None), P("chan", None, None)),
        check_vma=False,
    )
```

```python
import functools

import jax
import jax.numpy as jnp
from jax import lax
from jax.experimental import pallas as pl
from jax.experimental.pallas import tpu as pltpu
from jax.sharding import PartitionSpec as P

F32 = jnp.float32
BF16 = jnp.bfloat16
OFFSETS = [(a, b, c) for a in (-1, 0, 1) for b in (-1, 0, 1) for c in (-1, 0, 1)]
NT = (((1,), (1,)), ((), ()))
CUBE = 1616
WIDE = 640
VMEM = pl.BlockSpec(memory_space=pltpu.VMEM)
SMEM = pl.BlockSpec(memory_space=pltpu.SMEM)
PARAMS = pltpu.CompilerParams(vmem_limit_bytes=48 * 1024 * 1024)


def spans(shift):
    if shift < 0:
        return [(0, 7)]
    if shift > 0:
        return [(9, 0)]
    return [(1 + i, i) for i in range(8)]


def fill_cube(slots, block, voxels, cube, base):
    for number, (a, b, c) in enumerate(OFFSETS):
        first = pl.multiple_of(slots[block, number] * 512, 512)
        for i_to, i_from in spans(a):
            if c == 0:
                for j_to, j_from in spans(b):
                    row = base + (i_to * 10 + j_to) * 16 + 8
                    cube[row : row + 8, :] = voxels[pl.ds(first + i_from * 64 + j_from * 8, 8), :]
                continue
            k_from, k_to = (7, 7) if c < 0 else (0, 16)
            if b == 0:
                source = pl.ds(first + i_from * 64 + k_from, 8, stride=8)
                cube[pl.ds(base + (i_to * 10 + 1) * 16 + k_to, 8, stride=16), :] = voxels[source, :]
            else:
                ((j_to, j_from),) = spans(b)
                row = base + (i_to * 10 + j_to) * 16 + k_to
                source = pl.ds(first + i_from * 64 + j_from * 8 + k_from, 1)
                cube[row : row + 1, :] = voxels[source, :]


def pack_patches(cube, base, patches, top):
    for i in range(10):
        for c in range(3):
            rows = [
                cube[base + (i * 10 + j) * 16 + 7 + c : base + (i * 10 + j) * 16 + 15 + c, :]
                for j in range(10)
            ]
            pairs = [
                jnp.concatenate([rows[j], rows[j + 1]], axis=0).astype(BF16) for j in range(9)
            ]
            for b in range(3):
                lanes = (3 * b + c) * 128
                for t in range(4):
                    row = top + i * 64 + t * 16
                    patches[row : row + 16, lanes : lanes + 128] = pairs[2 * t + b]


def stack_weight(weight, stacked):
    out = weight.shape[1]
    for number in range(27):
        a, lanes = number // 9, number % 9 * 128
        stacked[a * out : (a + 1) * out, lanes : lanes + 128] = weight[number]


def forward_kernel(
    blocks, slots, gathered, weight, cotangent, occupancy,
    activation, stacked, grads, tiles,
    voxels, cube, patches,
):
    stack_weight(weight, stacked)
    for slot in range(blocks + 2):
        block = jnp.concatenate([gathered[c, slot] for c in range(gathered.shape[0])], axis=0)
        voxels[slot * 512 : (slot + 1) * 512, :] = block.astype(F32).T
    voxels[(blocks + 2) * 512 : (blocks + 3) * 512, :] = jnp.zeros((512, 128), F32)
    for p in range(blocks):
        fill_cube(slots, p, voxels, cube, p * CUBE)
        pack_patches(cube, p * CUBE, patches, p * WIDE)
        wide = lax.dot_general(
            stacked[...], patches[p * WIDE : (p + 1) * WIDE, :], NT, preferred_element_type=F32
        )
        pre = (
            wide[0:64, 0:512]
            + pltpu.roll(wide[64:128], WIDE - 64, 1)[:, 0:512]
            + wide[128:192, 128:640]
        )
        live = occupancy[p : p + 1, :].astype(F32)
        sigma = jax.nn.sigmoid(pre)
        activation[p] = (pre * sigma * live).astype(BF16)
        slope = sigma * (1.0 + pre * (1.0 - sigma))
        grad = (cotangent[p].astype(F32) * slope * live).astype(BF16).astype(F32)
        grad = jnp.concatenate([grad, jnp.zeros((64, 128), F32)], axis=1)
        lanes = slice(p * WIDE, (p + 1) * WIDE)
        grads[0:64, lanes] = grad.astype(BF16)
        grads[64:128, lanes] = pltpu.roll(grad, 64, 1).astype(BF16)
        grads[128:192, lanes] = pltpu.roll(grad, 128, 1).astype(BF16)
    for first in range(0, 9, 2):
        count = min(2, 9 - first)
        part = jnp.dot(
            grads[...],
            patches[:, first * 128 : (first + count) * 128],
            preferred_element_type=F32,
        )
        for t in range(count):
            for r in range(12):
                corner = part[r * 16 : (r + 1) * 16, t * 128 : (t + 1) * 128]
                tiles[(r // 4 * 9 + first + t) * 4 + r % 4] = corner.astype(BF16)
    for t in range(108, tiles.shape[0]):
        tiles[t] = jnp.zeros((16, 128), BF16)


def backward_kernel(
    blocks, slots, stacked, grads, pieces, sums, wide
):
    sums[...] = jnp.zeros_like(sums)
    row_index = lax.broadcasted_iota(jnp.int32, (64, 128), 0) % 8
    edge = lax.broadcasted_iota(jnp.int32, (8, 128), 0)
    for p in range(blocks):
        turn = grads[:, p * WIDE : (p + 1) * WIDE].astype(F32).T.astype(BF16)
        wide[...] = jnp.dot(turn, stacked[...], preferred_element_type=F32)
        for i in range(10):
            a, i_to = (-1, 7) if i == 0 else ((1, 0) if i == 9 else (0, i - 1))

            def line(j, c):
                total = None
                for b in range(3):
                    if 0 <= j - b < 8:
                        row = i * 64 + (j - b) * 8
                        lanes = (3 * b + c) * 128
                        term = wide[row : row + 8, lanes : lanes + 128]
                        total = term if total is None else total + term
                return total

            for b, js in ((-1, [0]), (0, list(range(1, 9))), (1, [9])):
                before = [pltpu.roll(line(j, 0), 7, 0) for j in js]
                centre = [line(j, 1) for j in js]
                after = [pltpu.roll(line(j, 2), 1, 0) for j in js]
                j_to = 7 if b < 0 else 0
                for c in (-1, 0, 1):
                    if c < 0:
                        parts = [jnp.where(edge == 7, x, 0.0) for x in before]
                    elif c > 0:
                        parts = [jnp.where(edge == 0, x, 0.0) for x in after]
                    else:
                        parts = [
                            y + jnp.where(edge < 7, x, 0.0) + jnp.where(edge > 0, z, 0.0)
                            for x, y, z in zip(before, centre, after)
                        ]
                    part = parts[0] if len(parts) == 1 else jnp.concatenate(parts, axis=0)
                    number = 9 * (a + 1) + 3 * (b + 1) + c + 1
                    first = pl.multiple_of(slots[p, number] * 512, 512)
                    rows = pl.ds(first + i_to * 64 + j_to * 8, 8 * len(js))
                    sums[rows, :] = sums[rows, :] + part
    share = pieces.shape[2]
    for slot in range(blocks + 2):
        turned = sums[slot * 512 : (slot + 1) * 512, :].T.astype(BF16)
        for c in range(pieces.shape[0]):
            pieces[c, slot] = turned[c * share : (c + 1) * share, :]


def shape(*dims, dtype=BF16):
    return jax.ShapeDtypeStruct(dims, dtype)


def call_forward(slots, gathered, weight, cotangent, occupancy, tiles):
    blocks, out = cotangent.shape[:2]
    return pl.pallas_call(
        functools.partial(forward_kernel, blocks),
        out_shape=[
            shape(blocks, out, 512),
            shape(3 * out, 1152),
            shape(3 * out, blocks * WIDE),
            shape(tiles, 16, 128),
        ],
        in_specs=[SMEM] + [VMEM] * 4,
        out_specs=[VMEM] * 4,
        scratch_shapes=[
            pltpu.VMEM(((blocks + 3) * 512, 128), F32),
            pltpu.VMEM((blocks * CUBE, 128), F32),
            pltpu.VMEM((blocks * WIDE, 1152), BF16),
        ],
        compiler_params=PARAMS,
    )(slots, gathered, weight, cotangent, occupancy)


def call_backward(slots, stacked, grads, chan):
    blocks = slots.shape[0]
    share = 128 // chan
    return pl.pallas_call(
        functools.partial(backward_kernel, blocks),
        out_shape=shape(chan, blocks + 2, share, 512),
        in_specs=[SMEM, VMEM, VMEM],
        out_specs=VMEM,
        scratch_shapes=[
            pltpu.VMEM(((blocks + 3) * 512, 128), F32),
            pltpu.VMEM((WIDE, 1152), F32),
        ],
        compiler_params=PARAMS,
    )(slots, stacked, grads)


def add_kernel(copies, pieces, out):
    total = pieces[0].astype(F32)
    for n in range(1, pieces.shape[0]):
        total = total + pieces[n].astype(F32)
    for n in range(copies):
        out[n] = total.astype(BF16)


def call_add(pieces, copies):
    return pl.pallas_call(
        functools.partial(add_kernel, copies),
        out_shape=shape(copies, *pieces.shape[1:]),
        in_specs=[VMEM],
        out_specs=VMEM,
        compiler_params=PARAMS,
    )(pieces)


def sum_kernel(blocks, pieces, own, to_partner, to_across):
    for slot in range(blocks + 2):
        total = pieces[0, slot].astype(F32)
        for c in range(1, pieces.shape[0]):
            total = total + pieces[c, slot].astype(F32)
        if slot < blocks:
            own[slot] = total
        else:
            (to_partner if slot == blocks else to_across)[...] = total.astype(BF16)


def call_sum(pieces):
    blocks, rim = pieces.shape[1] - 2, pieces.shape[2:]
    return pl.pallas_call(
        functools.partial(sum_kernel, blocks),
        out_shape=[shape(blocks, *rim, dtype=F32), shape(*rim), shape(*rim)],
        in_specs=[VMEM],
        out_specs=[VMEM] * 3,
        compiler_params=PARAMS,
    )(pieces)


def final_kernel(even, own, from_partner, from_across, occupancy, out):
    blocks = own.shape[0]
    is_even = even[0] == 1
    partner, across = from_partner[...].astype(F32), from_across[...].astype(F32)
    for slot in range(blocks):
        total = own[slot]
        if slot == 0:
            total = total + jnp.where(is_even, across, partner)
        if slot == blocks - 1:
            total = total + jnp.where(is_even, partner, across)
        out[slot] = (total * occupancy[slot : slot + 1, :].astype(F32)).astype(BF16)


def call_final(even, own, from_partner, from_across, occupancy):
    return pl.pallas_call(
        final_kernel,
        out_shape=shape(*own.shape),
        in_specs=[SMEM] + [VMEM] * 4,
        out_specs=VMEM,
        compiler_params=PARAMS,
    )(even.astype(jnp.int32).reshape(1), own, from_partner, from_across, occupancy)


def stages_of(count):
    return {128: (4, 16, 2), 4: (2, 1, 2), 8: (2, 2, 2), 16: (2, 4, 2)}[count]


def exchange(pieces, groups):
    return lax.all_to_all(pieces, "space", 0, 0, axis_index_groups=groups)


def groups_of(space):
    columns, rows, cores = stages_of(space)
    near, far = {}, {}
    for index in range(space):
        y, z, core = index // (rows * cores), index // cores % rows, index % cores
        near.setdefault(z // 2, []).append(index)
        far.setdefault((y, core, z % 2), []).append(index)
    return list(near.values()), list(far.values())


def on_device(features, occupancy, weight, cotangent, neighbours):
    blocks = features.shape[0]
    out = weight.shape[0]
    space = lax.axis_size("space")
    chan = lax.axis_size("chan")
    near, far = groups_of(space)
    share = -(-108 // len(near[0]))
    place = lax.axis_index("space")
    even = place % 2 == 0

    partner = [(i, i ^ 1) for i in range(space)]
    across = [(i, i - 1 if i % 2 == 0 else i + 1) for i in range(1, space - 1)]
    masked = features * occupancy.astype(BF16)[:, None, :]
    first, last = masked[0], masked[blocks - 1]
    from_partner = lax.ppermute(jnp.where(even, last, first), "space", partner)
    from_across = lax.ppermute(jnp.where(even, first, last), "space", across)
    held = jnp.concatenate([masked, from_partner[None], from_across[None]])
    gathered = lax.all_gather(held, "chan", axis=0)

    ids = jnp.concatenate(
        [
            neighbours[:, :13],
            (place * blocks + jnp.arange(blocks, dtype=jnp.int32))[:, None],
            neighbours[:, 13:],
        ],
        axis=1,
    )
    slots = ids - place * blocks
    below = jnp.where(even, blocks + 1, blocks)
    above = jnp.where(even, blocks, blocks + 1)
    slots = jnp.where(slots == -1, below, jnp.where(slots == blocks, above, slots))
    slots = jnp.where(ids < 0, blocks + 2, slots)

    activation, stacked, grads, tiles = call_forward(
        slots, gathered, jnp.transpose(weight, (1, 0, 2)), cotangent, occupancy,
        len(near[0]) * share,
    )

    pieces = call_backward(slots, stacked, grads, chan)
    own, rim_partner, rim_across = call_sum(lax.all_to_all(pieces, "chan", 0, 0))
    rim_partner, rim_across, tiles = lax.optimization_barrier((rim_partner, rim_across, tiles))
    to_partner = lax.ppermute(rim_partner, "space", partner)
    to_across = lax.ppermute(rim_across, "space", across)

    parts = exchange(tiles.reshape(len(near[0]), share, 16, 128), near)
    to_partner, to_across, parts = lax.optimization_barrier((to_partner, to_across, parts))
    parts = exchange(call_add(parts, len(far[0])), far)
    total = exchange(call_add(parts, len(near[0])), near)
    total = total.reshape(-1, 16, 128)[:108].astype(F32).reshape(27, out, 128)
    weight_grad = jnp.transpose(total * lax.rsqrt(F32(space * blocks * 512)), (1, 0, 2))

    input_grad = call_final(even, own, to_partner, to_across, occupancy)
    return (activation, input_grad, weight_grad)


def solution(mesh):
    placed = (
        P("space", "chan", None),
        P("space", None),
        P("chan", None, None),
        P("space", "chan", None),
        P("space", None),
    )
    return jax.shard_map(
        on_device,
        mesh=mesh,
        in_specs=placed,
        out_specs=(P("space", "chan", None), P("space", "chan", None), P("chan", None, None)),
        check_vma=False,
    )
```

```python
import functools

import jax
import jax.numpy as jnp
from jax import lax
from jax.experimental import pallas as pl
from jax.experimental.pallas import tpu as pltpu
from jax.sharding import PartitionSpec as P

F32 = jnp.float32
BF16 = jnp.bfloat16
OFFSETS = [(a, b, c) for a in (-1, 0, 1) for b in (-1, 0, 1) for c in (-1, 0, 1)]
NT = (((1,), (1,)), ((), ()))
CUBE = 1616
WIDE = 640
VMEM = pl.BlockSpec(memory_space=pltpu.VMEM)
SMEM = pl.BlockSpec(memory_space=pltpu.SMEM)
PARAMS = pltpu.CompilerParams(vmem_limit_bytes=48 * 1024 * 1024)


def spans(shift):
    if shift < 0:
        return [(0, 7)]
    if shift > 0:
        return [(9, 0)]
    return [(1 + i, i) for i in range(8)]


def fill_cube(slots, block, voxels, cube, base):
    for number, (a, b, c) in enumerate(OFFSETS):
        first = pl.multiple_of(slots[block, number] * 512, 512)
        for i_to, i_from in spans(a):
            if c == 0:
                for j_to, j_from in spans(b):
                    row = base + (i_to * 10 + j_to) * 16 + 8
                    cube[row : row + 8, :] = voxels[pl.ds(first + i_from * 64 + j_from * 8, 8), :]
                continue
            k_from, k_to = (7, 7) if c < 0 else (0, 16)
            if b == 0:
                source = pl.ds(first + i_from * 64 + k_from, 8, stride=8)
                cube[pl.ds(base + (i_to * 10 + 1) * 16 + k_to, 8, stride=16), :] = voxels[source, :]
            else:
                ((j_to, j_from),) = spans(b)
                row = base + (i_to * 10 + j_to) * 16 + k_to
                source = pl.ds(first + i_from * 64 + j_from * 8 + k_from, 1)
                cube[row : row + 1, :] = voxels[source, :]


def pack_patches(cube, base, patches, top):
    for i in range(10):
        for c in range(3):
            rows = [
                cube[base + (i * 10 + j) * 16 + 7 + c : base + (i * 10 + j) * 16 + 15 + c, :]
                for j in range(10)
            ]
            pairs = [
                jnp.concatenate([rows[j], rows[j + 1]], axis=0).astype(BF16) for j in range(9)
            ]
            for b in range(3):
                lanes = (3 * b + c) * 128
                for t in range(4):
                    row = top + i * 64 + t * 16
                    patches[row : row + 16, lanes : lanes + 128] = pairs[2 * t + b]


def stack_weight(weight, stacked):
    out = weight.shape[1]
    for number in range(27):
        a, lanes = number // 9, number % 9 * 128
        stacked[a * out : (a + 1) * out, lanes : lanes + 128] = weight[number]


def forward_kernel(
    blocks, slots, gathered, weight, cotangent, occupancy,
    activation, stacked, grads, tiles,
    voxels, cube, patches,
):
    stack_weight(weight, stacked)
    for slot in range(blocks + 2):
        block = jnp.concatenate([gathered[c, slot] for c in range(gathered.shape[0])], axis=0)
        voxels[slot * 512 : (slot + 1) * 512, :] = block.astype(F32).T
    voxels[(blocks + 2) * 512 : (blocks + 3) * 512, :] = jnp.zeros((512, 128), F32)
    for p in range(blocks):
        fill_cube(slots, p, voxels, cube, p * CUBE)
        pack_patches(cube, p * CUBE, patches, p * WIDE)
        wide = lax.dot_general(
            stacked[...], patches[p * WIDE : (p + 1) * WIDE, :], NT, preferred_element_type=F32
        )
        pre = (
            wide[0:64, 0:512]
            + pltpu.roll(wide[64:128], WIDE - 64, 1)[:, 0:512]
            + wide[128:192, 128:640]
        )
        live = occupancy[p : p + 1, :].astype(F32)
        sigma = jax.nn.sigmoid(pre)
        activation[p] = (pre * sigma * live).astype(BF16)
        slope = sigma * (1.0 + pre * (1.0 - sigma))
        grad = (cotangent[p].astype(F32) * slope * live).astype(BF16).astype(F32)
        grad = jnp.concatenate([grad, jnp.zeros((64, 128), F32)], axis=1)
        lanes = slice(p * WIDE, (p + 1) * WIDE)
        grads[0:64, lanes] = grad.astype(BF16)
        grads[64:128, lanes] = pltpu.roll(grad, 64, 1).astype(BF16)
        grads[128:192, lanes] = pltpu.roll(grad, 128, 1).astype(BF16)
    for first in range(0, 9, 2):
        count = min(2, 9 - first)
        part = jnp.dot(
            grads[...],
            patches[:, first * 128 : (first + count) * 128],
            preferred_element_type=F32,
        )
        for t in range(count):
            for r in range(12):
                corner = part[r * 16 : (r + 1) * 16, t * 128 : (t + 1) * 128]
                tiles[(r // 4 * 9 + first + t) * 4 + r % 4] = corner.astype(BF16)
    for t in range(108, tiles.shape[0]):
        tiles[t] = jnp.zeros((16, 128), BF16)


def backward_kernel(
    blocks, slots, place, stacked, grads, mine, *rest
):
    sends, (sums, wide, turned) = rest[:-3], rest[-3:]
    sums[...] = jnp.zeros_like(sums)
    edge = lax.broadcasted_iota(jnp.int32, (8, 128), 0)
    for p in range(blocks):
        turn = grads[:, p * WIDE : (p + 1) * WIDE].astype(F32).T.astype(BF16)
        wide[...] = jnp.dot(turn, stacked[...], preferred_element_type=F32)
        for i in range(10):
            a, i_to = (-1, 7) if i == 0 else ((1, 0) if i == 9 else (0, i - 1))

            def line(j, c):
                total = None
                for b in range(3):
                    if 0 <= j - b < 8:
                        row = i * 64 + (j - b) * 8
                        lanes = (3 * b + c) * 128
                        term = wide[row : row + 8, lanes : lanes + 128]
                        total = term if total is None else total + term
                return total

            for b, js in ((-1, [0]), (0, list(range(1, 9))), (1, [9])):
                before = [pltpu.roll(line(j, 0), 7, 0) for j in js]
                centre = [line(j, 1) for j in js]
                after = [pltpu.roll(line(j, 2), 1, 0) for j in js]
                j_to = 7 if b < 0 else 0
                for c in (-1, 0, 1):
                    if c < 0:
                        parts = [jnp.where(edge == 7, x, 0.0) for x in before]
                    elif c > 0:
                        parts = [jnp.where(edge == 0, x, 0.0) for x in after]
                    else:
                        parts = [
                            y + jnp.where(edge < 7, x, 0.0) + jnp.where(edge > 0, z, 0.0)
                            for x, y, z in zip(before, centre, after)
                        ]
                    part = parts[0] if len(parts) == 1 else jnp.concatenate(parts, axis=0)
                    number = 9 * (a + 1) + 3 * (b + 1) + c + 1
                    first = pl.multiple_of(slots[p, number] * 512, 512)
                    rows = pl.ds(first + i_to * 64 + j_to * 8, 8 * len(js))
                    sums[rows, :] = sums[rows, :] + part
    count, share = len(sends) + 1, mine.shape[1]
    for slot in range(blocks + 2):
        turned[slot * 128 : (slot + 1) * 128, :] = sums[slot * 512 : (slot + 1) * 512, :].T
    for shift in range(count):
        row = pl.multiple_of(lax.rem(place[0] + shift, count) * share, share)
        for slot in range(blocks + 2):
            piece = turned[pl.ds(slot * 128 + row, share), :]
            if shift == 0:
                mine[slot] = piece
            else:
                sends[shift - 1][slot] = piece.astype(BF16)


def shape(*dims, dtype=BF16):
    return jax.ShapeDtypeStruct(dims, dtype)


def call_forward(slots, gathered, weight, cotangent, occupancy, tiles):
    blocks, out = cotangent.shape[:2]
    return pl.pallas_call(
        functools.partial(forward_kernel, blocks),
        out_shape=[
            shape(blocks, out, 512),
            shape(3 * out, 1152),
            shape(3 * out, blocks * WIDE),
            shape(tiles, 16, 128),
        ],
        in_specs=[SMEM] + [VMEM] * 4,
        out_specs=[VMEM] * 4,
        scratch_shapes=[
            pltpu.VMEM(((blocks + 3) * 512, 128), F32),
            pltpu.VMEM((blocks * CUBE, 128), F32),
            pltpu.VMEM((blocks * WIDE, 1152), BF16),
        ],
        compiler_params=PARAMS,
        cost_estimate=pl.CostEstimate(flops=3 * 10**9, bytes_accessed=4 * 10**6, transcendentals=10**6),
    )(slots, gathered, weight, cotangent, occupancy)


def call_backward(slots, place, stacked, grads, chan):
    blocks = slots.shape[0]
    piece = (blocks + 2, 128 // chan, 512)
    return pl.pallas_call(
        functools.partial(backward_kernel, blocks),
        out_shape=[shape(*piece, dtype=F32)] + [shape(*piece)] * (chan - 1),
        in_specs=[SMEM, SMEM, VMEM, VMEM],
        out_specs=[VMEM] * chan,
        scratch_shapes=[
            pltpu.VMEM(((blocks + 3) * 512, 128), F32),
            pltpu.VMEM((WIDE, 1152), F32),
            pltpu.VMEM(((blocks + 2) * 128, 512), F32),
        ],
        compiler_params=PARAMS,
        cost_estimate=pl.CostEstimate(flops=2 * 10**9, bytes_accessed=8 * 10**6, transcendentals=0),
    )(slots, place, stacked, grads)


def add_kernel(copies, pieces, out):
    total = pieces[0].astype(F32)
    for n in range(1, pieces.shape[0]):
        total = total + pieces[n].astype(F32)
    for n in range(copies):
        out[n] = total.astype(BF16)


def call_add(pieces, copies):
    return pl.pallas_call(
        functools.partial(add_kernel, copies),
        out_shape=shape(copies, *pieces.shape[1:]),
        in_specs=[VMEM],
        out_specs=VMEM,
        compiler_params=PARAMS,
    )(pieces)


def sum_kernel(blocks, mine, *refs):
    arrived, (own, to_partner, to_across) = refs[:-3], refs[-3:]
    for slot in range(blocks + 2):
        total = mine[slot]
        for ref in arrived:
            total = total + ref[slot].astype(F32)
        if slot < blocks:
            own[slot] = total
        else:
            (to_partner if slot == blocks else to_across)[...] = total.astype(BF16)


def call_sum(mine, arrived):
    blocks, rim = mine.shape[0] - 2, mine.shape[1:]
    return pl.pallas_call(
        functools.partial(sum_kernel, blocks),
        out_shape=[shape(blocks, *rim, dtype=F32), shape(*rim), shape(*rim)],
        in_specs=[VMEM] * (1 + len(arrived)),
        out_specs=[VMEM] * 3,
        compiler_params=PARAMS,
    )(mine, *arrived)


def final_kernel(even, own, from_partner, from_across, occupancy, out):
    blocks = own.shape[0]
    is_even = even[0] == 1
    partner, across = from_partner[...].astype(F32), from_across[...].astype(F32)
    for slot in range(blocks):
        total = own[slot]
        if slot == 0:
            total = total + jnp.where(is_even, across, partner)
        if slot == blocks - 1:
            total = total + jnp.where(is_even, partner, across)
        out[slot] = (total * occupancy[slot : slot + 1, :].astype(F32)).astype(BF16)


def call_final(even, own, from_partner, from_across, occupancy):
    return pl.pallas_call(
        final_kernel,
        out_shape=shape(*own.shape),
        in_specs=[SMEM] + [VMEM] * 4,
        out_specs=VMEM,
        compiler_params=PARAMS,
    )(even.astype(jnp.int32).reshape(1), own, from_partner, from_across, occupancy)


def stages_of(count):
    return {128: (4, 16, 2), 4: (2, 1, 2), 8: (2, 2, 2), 16: (2, 4, 2)}[count]


def exchange(pieces, groups):
    return lax.all_to_all(pieces, "space", 0, 0, axis_index_groups=groups)


def groups_of(space):
    columns, rows, cores = stages_of(space)
    near, far = {}, {}
    for index in range(space):
        y, z, core = index // (rows * cores), index // cores % rows, index % cores
        near.setdefault(z // 2, []).append(index)
        far.setdefault((y, core, z % 2), []).append(index)
    return list(near.values()), list(far.values())


def on_device(features, occupancy, weight, cotangent, neighbours):
    blocks = features.shape[0]
    out = weight.shape[0]
    space = lax.axis_size("space")
    chan = lax.axis_size("chan")
    near, far = groups_of(space)
    share = -(-108 // len(near[0]))
    place = lax.axis_index("space")
    even = place % 2 == 0

    partner = [(i, i ^ 1) for i in range(space)]
    across = [(i, i - 1 if i % 2 == 0 else i + 1) for i in range(1, space - 1)]
    masked = features * occupancy.astype(BF16)[:, None, :]
    first, last = masked[0], masked[blocks - 1]
    from_partner = lax.ppermute(jnp.where(even, last, first), "space", partner)
    from_across = lax.ppermute(jnp.where(even, first, last), "space", across)
    held = jnp.concatenate([masked, from_partner[None], from_across[None]])
    gathered = lax.all_gather(held, "chan", axis=0)

    ids = jnp.concatenate(
        [
            neighbours[:, :13],
            (place * blocks + jnp.arange(blocks, dtype=jnp.int32))[:, None],
            neighbours[:, 13:],
        ],
        axis=1,
    )
    slots = ids - place * blocks
    below = jnp.where(even, blocks + 1, blocks)
    above = jnp.where(even, blocks, blocks + 1)
    slots = jnp.where(slots == -1, below, jnp.where(slots == blocks, above, slots))
    slots = jnp.where(ids < 0, blocks + 2, slots)

    activation, stacked, grads, tiles = call_forward(
        slots, gathered, jnp.transpose(weight, (1, 0, 2)), cotangent, occupancy,
        len(near[0]) * share,
    )

    parts = exchange(tiles.reshape(len(near[0]), share, 16, 128), near)
    mine, *sends = call_backward(
        slots, lax.axis_index("chan").astype(jnp.int32).reshape(1), stacked, grads, chan
    )
    parts, mine, sends = lax.optimization_barrier((parts, mine, sends))
    parts = exchange(call_add(parts, len(far[0])), far)
    arrived = [
        lax.ppermute(piece, "chan", [(c, (c + shift + 1) % chan) for c in range(chan)])
        for shift, piece in enumerate(sends)
    ]
    parts, arrived = lax.optimization_barrier((parts, arrived))
    total = exchange(call_add(parts, len(near[0])), near)
    own, rim_partner, rim_across = call_sum(mine, arrived)
    to_partner = lax.ppermute(rim_partner, "space", partner)
    to_across = lax.ppermute(rim_across, "space", across)
    total = total.reshape(-1, 16, 128)[:108].astype(F32).reshape(27, out, 128)
    weight_grad = jnp.transpose(total * lax.rsqrt(F32(space * blocks * 512)), (1, 0, 2))

    input_grad = call_final(even, own, to_partner, to_across, occupancy)
    return (activation, input_grad, weight_grad)


def solution(mesh):
    placed = (
        P("space", "chan", None),
        P("space", None),
        P("chan", None, None),
        P("space", "chan", None),
        P("space", None),
    )
    return jax.shard_map(
        on_device,
        mesh=mesh,
        in_specs=placed,
        out_specs=(P("space", "chan", None), P("space", "chan", None), P("chan", None, None)),
        check_vma=False,
    )
```

```python
import functools

import jax
import jax.numpy as jnp
from jax import lax
from jax.experimental import pallas as pl
from jax.experimental.pallas import tpu as pltpu
from jax.sharding import PartitionSpec as P

F32 = jnp.float32
BF16 = jnp.bfloat16
OFFSETS = [(a, b, c) for a in (-1, 0, 1) for b in (-1, 0, 1) for c in (-1, 0, 1)]
NT = (((1,), (1,)), ((), ()))
CUBE = 1616
WIDE = 640
VMEM = pl.BlockSpec(memory_space=pltpu.VMEM)
SMEM = pl.BlockSpec(memory_space=pltpu.SMEM)
PARAMS = pltpu.CompilerParams(vmem_limit_bytes=48 * 1024 * 1024)


def spans(shift):
    if shift < 0:
        return [(0, 7)]
    if shift > 0:
        return [(9, 0)]
    return [(1 + i, i) for i in range(8)]


def fill_cube(slots, block, voxels, cube, base):
    for number, (a, b, c) in enumerate(OFFSETS):
        first = pl.multiple_of(slots[block, number] * 512, 512)
        for i_to, i_from in spans(a):
            if c == 0:
                for j_to, j_from in spans(b):
                    row = base + (i_to * 10 + j_to) * 16 + 8
                    cube[row : row + 8, :] = voxels[pl.ds(first + i_from * 64 + j_from * 8, 8), :]
                continue
            k_from, k_to = (7, 7) if c < 0 else (0, 16)
            if b == 0:
                source = pl.ds(first + i_from * 64 + k_from, 8, stride=8)
                cube[pl.ds(base + (i_to * 10 + 1) * 16 + k_to, 8, stride=16), :] = voxels[source, :]
            else:
                ((j_to, j_from),) = spans(b)
                row = base + (i_to * 10 + j_to) * 16 + k_to
                source = pl.ds(first + i_from * 64 + j_from * 8 + k_from, 1)
                cube[row : row + 1, :] = voxels[source, :]


def pack_patches(cube, base, patches, top):
    for i in range(10):
        for c in range(3):
            rows = [
                cube[base + (i * 10 + j) * 16 + 7 + c : base + (i * 10 + j) * 16 + 15 + c, :]
                for j in range(10)
            ]
            pairs = [
                jnp.concatenate([rows[j], rows[j + 1]], axis=0).astype(BF16) for j in range(9)
            ]
            for b in range(3):
                lanes = (3 * b + c) * 128
                for t in range(4):
                    row = top + i * 64 + t * 16
                    patches[row : row + 16, lanes : lanes + 128] = pairs[2 * t + b]


def load_block(gathered, occupancy, slot):
    block = jnp.concatenate([gathered[c, slot] for c in range(gathered.shape[0])], axis=0)
    return block.astype(F32) * occupancy[slot : slot + 1, :].astype(F32)


def rim_kernel(even, gathered, occupancy, to_partner, to_across):
    first = load_block(gathered, occupancy, 0).astype(BF16)
    last = load_block(gathered, occupancy, gathered.shape[1] - 1).astype(BF16)
    is_even = even[0] == 1
    to_partner[...] = jnp.where(is_even, last, first)
    to_across[...] = jnp.where(is_even, first, last)


def forward_block(
    slots, block, stacked, cotangent, occupancy, voxels, cube, patches, grads, place
):
    base, top = place * CUBE, place * WIDE
    fill_cube(slots, block, voxels, cube, base)
    pack_patches(cube, base, patches, top)
    wide = lax.dot_general(
        stacked[...], patches[top : top + WIDE, :], NT, preferred_element_type=F32
    )
    pre = (
        wide[0:64, 0:512]
        + pltpu.roll(wide[64:128], WIDE - 64, 1)[:, 0:512]
        + wide[128:192, 128:640]
    )
    live = occupancy[block : block + 1, :].astype(F32)
    sigma = jax.nn.sigmoid(pre)
    slope = sigma * (1.0 + pre * (1.0 - sigma))
    grad = (cotangent[block].astype(F32) * slope * live).astype(BF16).astype(F32)
    grad = jnp.concatenate([grad, jnp.zeros((64, 128), F32)], axis=1)
    lanes = slice(top, top + WIDE)
    grads[0:64, lanes] = grad.astype(BF16)
    grads[64:128, lanes] = pltpu.roll(grad, 64, 1).astype(BF16)
    grads[128:192, lanes] = pltpu.roll(grad, 128, 1).astype(BF16)
    return (pre * sigma * live).astype(BF16)


def own_voxels(gathered, occupancy, voxels):
    blocks = gathered.shape[1]
    for slot in range(blocks):
        block = load_block(gathered, occupancy, slot)
        voxels[slot * 512 : (slot + 1) * 512, :] = block.T
    voxels[(blocks + 2) * 512 : (blocks + 3) * 512, :] = jnp.zeros((512, 128), F32)


def inner_kernel(
    slots, gathered, weight, cotangent, occupancy,
    activation, stacked, grads, product,
    voxels, cube, patches,
):
    blocks = cotangent.shape[0]
    out = weight.shape[1]
    for number in range(27):
        a, lanes = number // 9, number % 9 * 128
        stacked[a * out : (a + 1) * out, lanes : lanes + 128] = weight[number]
    own_voxels(gathered, occupancy, voxels)
    for block in range(1, blocks - 1):
        activation[block - 1] = forward_block(
            slots, block, stacked, cotangent, occupancy, voxels, cube, patches, grads, block - 1
        )
    for first in range(0, 9, 2):
        lanes = slice(first * 128, min(first + 2, 9) * 128)
        product[:, lanes] = jnp.dot(grads[...], patches[:, lanes], preferred_element_type=F32)


def outer_kernel(
    slots, gathered, from_partner, from_across, cotangent, occupancy, inner, stacked, product,
    activation, grads, tiles,
    voxels, cube, patches,
):
    blocks = cotangent.shape[0]
    own_voxels(gathered, occupancy, voxels)
    for slot, rim in ((blocks, from_partner), (blocks + 1, from_across)):
        voxels[slot * 512 : (slot + 1) * 512, :] = rim[...].astype(F32).T
    activation[1 : blocks - 1] = inner[...]
    for place, block in enumerate((0, blocks - 1)):
        activation[block] = forward_block(
            slots, block, stacked, cotangent, occupancy, voxels, cube, patches, grads, place
        )
    for first in range(0, 9, 2):
        count = min(2, 9 - first)
        lanes = slice(first * 128, (first + count) * 128)
        part = product[:, lanes] + jnp.dot(
            grads[...], patches[:, lanes], preferred_element_type=F32
        )
        for t in range(count):
            for r in range(12):
                corner = part[r * 16 : (r + 1) * 16, t * 128 : (t + 1) * 128]
                tiles[(r // 4 * 9 + first + t) * 4 + r % 4] = corner.astype(BF16)
    for t in range(108, tiles.shape[0]):
        tiles[t] = jnp.zeros((16, 128), BF16)


def backward_kernel(
    blocks, slots, place, stacked, inner, outer, mine, *rest
):
    sends, (sums, wide, turned) = rest[:-3], rest[-3:]
    sums[...] = jnp.zeros_like(sums)
    edge = lax.broadcasted_iota(jnp.int32, (8, 128), 0)
    for p in range(blocks):
        grads, at = (inner, p - 1) if 0 < p < blocks - 1 else (outer, min(p, 1))
        turn = grads[:, at * WIDE : (at + 1) * WIDE].astype(F32).T.astype(BF16)
        wide[...] = jnp.dot(turn, stacked[...], preferred_element_type=F32)
        for i in range(10):
            a, i_to = (-1, 7) if i == 0 else ((1, 0) if i == 9 else (0, i - 1))

            def line(j, c):
                total = None
                for b in range(3):
                    if 0 <= j - b < 8:
                        row = i * 64 + (j - b) * 8
                        lanes = (3 * b + c) * 128
                        term = wide[row : row + 8, lanes : lanes + 128]
                        total = term if total is None else total + term
                return total

            for b, js in ((-1, [0]), (0, list(range(1, 9))), (1, [9])):
                before = [pltpu.roll(line(j, 0), 7, 0) for j in js]
                centre = [line(j, 1) for j in js]
                after = [pltpu.roll(line(j, 2), 1, 0) for j in js]
                j_to = 7 if b < 0 else 0
                for c in (-1, 0, 1):
                    if c < 0:
                        parts = [jnp.where(edge == 7, x, 0.0) for x in before]
                    elif c > 0:
                        parts = [jnp.where(edge == 0, x, 0.0) for x in after]
                    else:
                        parts = [
                            y + jnp.where(edge < 7, x, 0.0) + jnp.where(edge > 0, z, 0.0)
                            for x, y, z in zip(before, centre, after)
                        ]
                    part = parts[0] if len(parts) == 1 else jnp.concatenate(parts, axis=0)
                    number = 9 * (a + 1) + 3 * (b + 1) + c + 1
                    first = pl.multiple_of(slots[p, number] * 512, 512)
                    rows = pl.ds(first + i_to * 64 + j_to * 8, 8 * len(js))
                    sums[rows, :] = sums[rows, :] + part
    count, share = len(sends) + 1, mine.shape[1]
    for slot in range(blocks + 2):
        turned[slot * 128 : (slot + 1) * 128, :] = sums[slot * 512 : (slot + 1) * 512, :].T
    for shift in range(count):
        row = pl.multiple_of(lax.rem(place[0] + shift, count) * share, share)
        for slot in range(blocks + 2):
            piece = turned[pl.ds(slot * 128 + row, share), :]
            if shift == 0:
                mine[slot] = piece
            else:
                sends[shift - 1][slot] = piece.astype(BF16)


def shape(*dims, dtype=BF16):
    return jax.ShapeDtypeStruct(dims, dtype)


def call_rims(even, gathered, occupancy):
    rim = shape(128, 512)
    return pl.pallas_call(
        rim_kernel,
        out_shape=[rim, rim],
        in_specs=[SMEM, VMEM, VMEM],
        out_specs=[VMEM] * 2,
        compiler_params=PARAMS,
        cost_estimate=pl.CostEstimate(flops=10**6, bytes_accessed=10**6, transcendentals=0),
    )(even, gathered, occupancy)


def scratch_of(blocks, count):
    return [
        pltpu.VMEM(((blocks + 3) * 512, 128), F32),
        pltpu.VMEM((count * CUBE, 128), F32),
        pltpu.VMEM((count * WIDE, 1152), BF16),
    ]


def call_inner(slots, gathered, weight, cotangent, occupancy):
    blocks, out = cotangent.shape[:2]
    return pl.pallas_call(
        inner_kernel,
        out_shape=[
            shape(blocks - 2, out, 512),
            shape(3 * out, 1152),
            shape(3 * out, (blocks - 2) * WIDE),
            shape(3 * out, 1152, dtype=F32),
        ],
        in_specs=[SMEM] + [VMEM] * 4,
        out_specs=[VMEM] * 4,
        scratch_shapes=scratch_of(blocks, blocks - 2),
        compiler_params=PARAMS,
        cost_estimate=pl.CostEstimate(flops=10**9, bytes_accessed=4 * 10**6, transcendentals=10**5),
    )(slots, gathered, weight, cotangent, occupancy)


def call_outer(slots, gathered, rims, cotangent, occupancy, inner, stacked, product, tiles):
    blocks, out = cotangent.shape[:2]
    return pl.pallas_call(
        outer_kernel,
        out_shape=[
            shape(blocks, out, 512),
            shape(3 * out, 2 * WIDE),
            shape(tiles, 16, 128),
        ],
        in_specs=[SMEM] + [VMEM] * 8,
        out_specs=[VMEM] * 3,
        scratch_shapes=scratch_of(blocks, 2),
        compiler_params=PARAMS,
        cost_estimate=pl.CostEstimate(flops=10**9, bytes_accessed=4 * 10**6, transcendentals=10**5),
    )(slots, gathered, *rims, cotangent, occupancy, inner, stacked, product)


def call_backward(slots, place, stacked, inner, outer, chan):
    blocks = slots.shape[0]
    piece = (blocks + 2, 128 // chan, 512)
    return pl.pallas_call(
        functools.partial(backward_kernel, blocks),
        out_shape=[shape(*piece, dtype=F32)] + [shape(*piece)] * (chan - 1),
        in_specs=[SMEM, SMEM, VMEM, VMEM, VMEM],
        out_specs=[VMEM] * chan,
        scratch_shapes=[
            pltpu.VMEM(((blocks + 3) * 512, 128), F32),
            pltpu.VMEM((WIDE, 1152), F32),
            pltpu.VMEM(((blocks + 2) * 128, 512), F32),
        ],
        compiler_params=PARAMS,
        cost_estimate=pl.CostEstimate(flops=2 * 10**9, bytes_accessed=8 * 10**6, transcendentals=0),
    )(slots, place, stacked, inner, outer)


def add_kernel(copies, pieces, out):
    total = pieces[0].astype(F32)
    for n in range(1, pieces.shape[0]):
        total = total + pieces[n].astype(F32)
    for n in range(copies):
        out[n] = total.astype(BF16)


def call_add(pieces, copies):
    return pl.pallas_call(
        functools.partial(add_kernel, copies),
        out_shape=shape(copies, *pieces.shape[1:]),
        in_specs=[VMEM],
        out_specs=VMEM,
        compiler_params=PARAMS,
    )(pieces)


def sum_kernel(blocks, mine, *refs):
    arrived, (own, to_partner, to_across) = refs[:-3], refs[-3:]
    for slot in range(blocks + 2):
        total = mine[slot]
        for ref in arrived:
            total = total + ref[slot].astype(F32)
        if slot < blocks:
            own[slot] = total
        else:
            (to_partner if slot == blocks else to_across)[...] = total.astype(BF16)


def call_sum(mine, arrived):
    blocks, rim = mine.shape[0] - 2, mine.shape[1:]
    return pl.pallas_call(
        functools.partial(sum_kernel, blocks),
        out_shape=[shape(blocks, *rim, dtype=F32), shape(*rim), shape(*rim)],
        in_specs=[VMEM] * (1 + len(arrived)),
        out_specs=[VMEM] * 3,
        compiler_params=PARAMS,
    )(mine, *arrived)


def final_kernel(even, own, from_partner, from_across, occupancy, out):
    blocks = own.shape[0]
    is_even = even[0] == 1
    partner, across = from_partner[...].astype(F32), from_across[...].astype(F32)
    for slot in range(blocks):
        total = own[slot]
        if slot == 0:
            total = total + jnp.where(is_even, across, partner)
        if slot == blocks - 1:
            total = total + jnp.where(is_even, partner, across)
        out[slot] = (total * occupancy[slot : slot + 1, :].astype(F32)).astype(BF16)


def call_final(even, own, from_partner, from_across, occupancy):
    return pl.pallas_call(
        final_kernel,
        out_shape=shape(*own.shape),
        in_specs=[SMEM] + [VMEM] * 4,
        out_specs=VMEM,
        compiler_params=PARAMS,
    )(even, own, from_partner, from_across, occupancy)


def stages_of(count):
    return {128: (4, 16, 2), 4: (2, 1, 2), 8: (2, 2, 2), 16: (2, 4, 2)}[count]


def exchange(pieces, groups):
    return lax.all_to_all(pieces, "space", 0, 0, axis_index_groups=groups)


def groups_of(space):
    columns, rows, cores = stages_of(space)
    near, far = {}, {}
    for index in range(space):
        y, z, core = index // (rows * cores), index // cores % rows, index % cores
        near.setdefault(z // 2, []).append(index)
        far.setdefault((y, core, z % 2), []).append(index)
    return list(near.values()), list(far.values())


def on_device(features, occupancy, weight, cotangent, neighbours):
    blocks = features.shape[0]
    out = weight.shape[0]
    space = lax.axis_size("space")
    chan = lax.axis_size("chan")
    near, far = groups_of(space)
    share = -(-108 // len(near[0]))
    place = lax.axis_index("space")
    even = place % 2 == 0

    partner = [(i, i ^ 1) for i in range(space)]
    across = [(i, i - 1 if i % 2 == 0 else i + 1) for i in range(1, space - 1)]
    even_flag = even.astype(jnp.int32).reshape(1)
    gathered = lax.all_gather(features, "chan", axis=0)
    rims = [
        lax.ppermute(rim, "space", pairs)
        for rim, pairs in zip(call_rims(even_flag, gathered, occupancy), (partner, across))
    ]

    ids = jnp.concatenate(
        [
            neighbours[:, :13],
            (place * blocks + jnp.arange(blocks, dtype=jnp.int32))[:, None],
            neighbours[:, 13:],
        ],
        axis=1,
    )
    slots = ids - place * blocks
    below = jnp.where(even, blocks + 1, blocks)
    above = jnp.where(even, blocks, blocks + 1)
    slots = jnp.where(slots == -1, below, jnp.where(slots == blocks, above, slots))
    slots = jnp.where(ids < 0, blocks + 2, slots)

    inner, stacked, inner_grads, product = call_inner(
        slots, gathered, jnp.transpose(weight, (1, 0, 2)), cotangent, occupancy
    )
    activation, outer_grads, tiles = call_outer(
        slots, gathered, rims, cotangent, occupancy, inner, stacked, product, len(near[0]) * share
    )

    parts = exchange(tiles.reshape(len(near[0]), share, 16, 128), near)
    mine, *sends = call_backward(
        slots, lax.axis_index("chan").astype(jnp.int32).reshape(1), stacked,
        inner_grads, outer_grads, chan,
    )
    rings = [[(c, (c + shift) % chan) for c in range(chan)] for shift in range(1, chan)]
    arrived = [lax.ppermute(sends[0], "chan", rings[0])]
    parts, mine, arrived, sends = lax.optimization_barrier((parts, mine, arrived, sends))
    parts = exchange(call_add(parts, len(far[0])), far)
    arrived += [lax.ppermute(piece, "chan", ring) for piece, ring in zip(sends[1:], rings[1:])]
    parts, arrived = lax.optimization_barrier((parts, arrived))
    total = exchange(call_add(parts, len(near[0])), near)
    own, rim_partner, rim_across = call_sum(mine, arrived)
    to_partner = lax.ppermute(rim_partner, "space", partner)
    to_across = lax.ppermute(rim_across, "space", across)
    total = total.reshape(-1, 16, 128)[:108].astype(F32).reshape(27, out, 128)
    weight_grad = jnp.transpose(total * lax.rsqrt(F32(space * blocks * 512)), (1, 0, 2))

    input_grad = call_final(even_flag, own, to_partner, to_across, occupancy)
    return (activation, input_grad, weight_grad)


def solution(mesh):
    placed = (
        P("space", "chan", None),
        P("space", None),
        P("chan", None, None),
        P("space", "chan", None),
        P("space", None),
    )
    return jax.shard_map(
        on_device,
        mesh=mesh,
        in_specs=placed,
        out_specs=(P("space", "chan", None), P("space", "chan", None), P("chan", None, None)),
        check_vma=False,
    )
```

```python
import functools

import jax
import jax.numpy as jnp
from jax import lax
from jax.experimental import pallas as pl
from jax.experimental.pallas import tpu as pltpu
from jax.sharding import PartitionSpec as P

F32 = jnp.float32
BF16 = jnp.bfloat16
OFFSETS = [(a, b, c) for a in (-1, 0, 1) for b in (-1, 0, 1) for c in (-1, 0, 1)]
NT = (((1,), (1,)), ((), ()))
CUBE = 1616
WIDE = 640
VMEM = pl.BlockSpec(memory_space=pltpu.VMEM)
SMEM = pl.BlockSpec(memory_space=pltpu.SMEM)
PARAMS = pltpu.CompilerParams(vmem_limit_bytes=48 * 1024 * 1024)


def spans(shift):
    if shift < 0:
        return [(0, 7)]
    if shift > 0:
        return [(9, 0)]
    return [(1 + i, i) for i in range(8)]


def slot_of(spot, listed, block, number, blocks):
    if number == 13:
        return block
    name = listed[block, number if number < 13 else number - 1]
    local = name - spot[0] * blocks
    is_even = spot[1] == 1
    below = jnp.where(is_even, blocks + 1, blocks)
    above = jnp.where(is_even, blocks, blocks + 1)
    local = jnp.where(local == -1, below, jnp.where(local == blocks, above, local))
    return jnp.where(name < 0, blocks + 2, local)


def fill_cube(spot, listed, block, blocks, voxels, cube, base):
    for number, (a, b, c) in enumerate(OFFSETS):
        first = pl.multiple_of(slot_of(spot, listed, block, number, blocks) * 512, 512)
        for i_to, i_from in spans(a):
            if c == 0:
                for j_to, j_from in spans(b):
                    row = base + (i_to * 10 + j_to) * 16 + 8
                    cube[row : row + 8, :] = voxels[pl.ds(first + i_from * 64 + j_from * 8, 8), :]
                continue
            k_from, k_to = (7, 7) if c < 0 else (0, 16)
            if b == 0:
                source = pl.ds(first + i_from * 64 + k_from, 8, stride=8)
                cube[pl.ds(base + (i_to * 10 + 1) * 16 + k_to, 8, stride=16), :] = voxels[source, :]
            else:
                ((j_to, j_from),) = spans(b)
                row = base + (i_to * 10 + j_to) * 16 + k_to
                source = pl.ds(first + i_from * 64 + j_from * 8 + k_from, 1)
                cube[row : row + 1, :] = voxels[source, :]


def pack_patches(cube, base, patches, top):
    for i in range(10):
        for c in range(3):
            rows = [
                cube[base + (i * 10 + j) * 16 + 7 + c : base + (i * 10 + j) * 16 + 15 + c, :]
                for j in range(10)
            ]
            pairs = [
                jnp.concatenate([rows[j], rows[j + 1]], axis=0).astype(BF16) for j in range(9)
            ]
            for b in range(3):
                lanes = (3 * b + c) * 128
                for t in range(4):
                    row = top + i * 64 + t * 16
                    patches[row : row + 16, lanes : lanes + 128] = pairs[2 * t + b]


def load_block(gathered, occupancy, slot):
    block = jnp.concatenate([gathered[c, slot] for c in range(gathered.shape[0])], axis=0)
    return block.astype(F32) * occupancy[slot : slot + 1, :].astype(F32)


def rim_kernel(spot, gathered, occupancy, to_partner, to_across):
    first = load_block(gathered, occupancy, 0).astype(BF16)
    last = load_block(gathered, occupancy, gathered.shape[1] - 1).astype(BF16)
    is_even = spot[1] == 1
    to_partner[...] = jnp.where(is_even, last, first)
    to_across[...] = jnp.where(is_even, first, last)


def forward_block(
    spot, listed, block, stacked, cotangent, occupancy, voxels, cube, patches, grads, place
):
    base, top = place * CUBE, place * WIDE
    fill_cube(spot, listed, block, cotangent.shape[0], voxels, cube, base)
    pack_patches(cube, base, patches, top)
    wide = lax.dot_general(
        stacked[...], patches[top : top + WIDE, :], NT, preferred_element_type=F32
    )
    pre = (
        wide[0:64, 0:512]
        + pltpu.roll(wide[64:128], WIDE - 64, 1)[:, 0:512]
        + wide[128:192, 128:640]
    )
    live = occupancy[block : block + 1, :].astype(F32)
    sigma = jax.nn.sigmoid(pre)
    slope = sigma * (1.0 + pre * (1.0 - sigma))
    grad = (cotangent[block].astype(F32) * slope * live).astype(BF16).astype(F32)
    grad = jnp.concatenate([grad, jnp.zeros((64, 128), F32)], axis=1)
    lanes = slice(top, top + WIDE)
    grads[0:64, lanes] = grad.astype(BF16)
    grads[64:128, lanes] = pltpu.roll(grad, 64, 1).astype(BF16)
    grads[128:192, lanes] = pltpu.roll(grad, 128, 1).astype(BF16)
    return (pre * sigma * live).astype(BF16)


def own_voxels(gathered, occupancy, voxels):
    blocks = gathered.shape[1]
    for slot in range(blocks):
        block = load_block(gathered, occupancy, slot)
        voxels[slot * 512 : (slot + 1) * 512, :] = block.T
    voxels[(blocks + 2) * 512 : (blocks + 3) * 512, :] = jnp.zeros((512, 128), F32)


def inner_kernel(
    spot, listed, gathered, weight, cotangent, occupancy,
    activation, stacked, grads, product,
    voxels, cube, patches,
):
    blocks = cotangent.shape[0]
    out = weight.shape[1]
    for number in range(27):
        a, lanes = number // 9, number % 9 * 128
        stacked[a * out : (a + 1) * out, lanes : lanes + 128] = weight[number]
    own_voxels(gathered, occupancy, voxels)
    for block in range(1, blocks - 1):
        activation[block - 1] = forward_block(
            spot, listed, block, stacked, cotangent, occupancy, voxels, cube, patches, grads,
            block - 1,
        )
    for first in range(0, 9, 2):
        lanes = slice(first * 128, min(first + 2, 9) * 128)
        product[:, lanes] = jnp.dot(grads[...], patches[:, lanes], preferred_element_type=F32)


def outer_kernel(
    spot, listed, gathered, from_partner, from_across, cotangent, occupancy, inner, stacked, product,
    activation, grads, tiles,
    voxels, cube, patches,
):
    blocks = cotangent.shape[0]
    own_voxels(gathered, occupancy, voxels)
    for slot, rim in ((blocks, from_partner), (blocks + 1, from_across)):
        voxels[slot * 512 : (slot + 1) * 512, :] = rim[...].astype(F32).T
    activation[1 : blocks - 1] = inner[...]
    for place, block in enumerate((0, blocks - 1)):
        activation[block] = forward_block(
            spot, listed, block, stacked, cotangent, occupancy, voxels, cube, patches, grads, place
        )
    for first in range(0, 9, 2):
        count = min(2, 9 - first)
        lanes = slice(first * 128, (first + count) * 128)
        part = product[:, lanes] + jnp.dot(
            grads[...], patches[:, lanes], preferred_element_type=F32
        )
        for t in range(count):
            for r in range(12):
                corner = part[r * 16 : (r + 1) * 16, t * 128 : (t + 1) * 128]
                tiles[(r // 4 * 9 + first + t) * 4 + r % 4] = corner.astype(BF16)
    for t in range(108, tiles.shape[0]):
        tiles[t] = jnp.zeros((16, 128), BF16)


def add_gradients(spot, listed, picked, blocks, stacked, grads, sums, wide):
    edge = lax.broadcasted_iota(jnp.int32, (8, 128), 0)
    for at, p in enumerate(picked):
        turn = grads[:, at * WIDE : (at + 1) * WIDE].astype(F32).T.astype(BF16)
        wide[...] = jnp.dot(turn, stacked[...], preferred_element_type=F32)
        for i in range(10):
            a, i_to = (-1, 7) if i == 0 else ((1, 0) if i == 9 else (0, i - 1))

            def line(j, c):
                total = None
                for b in range(3):
                    if 0 <= j - b < 8:
                        row = i * 64 + (j - b) * 8
                        lanes = (3 * b + c) * 128
                        term = wide[row : row + 8, lanes : lanes + 128]
                        total = term if total is None else total + term
                return total

            for b, js in ((-1, [0]), (0, list(range(1, 9))), (1, [9])):
                before = [pltpu.roll(line(j, 0), 7, 0) for j in js]
                centre = [line(j, 1) for j in js]
                after = [pltpu.roll(line(j, 2), 1, 0) for j in js]
                j_to = 7 if b < 0 else 0
                for c in (-1, 0, 1):
                    if c < 0:
                        parts = [jnp.where(edge == 7, x, 0.0) for x in before]
                    elif c > 0:
                        parts = [jnp.where(edge == 0, x, 0.0) for x in after]
                    else:
                        parts = [
                            y + jnp.where(edge < 7, x, 0.0) + jnp.where(edge > 0, z, 0.0)
                            for x, y, z in zip(before, centre, after)
                        ]
                    part = parts[0] if len(parts) == 1 else jnp.concatenate(parts, axis=0)
                    number = 9 * (a + 1) + 3 * (b + 1) + c + 1
                    slot = slot_of(spot, listed, p, number, blocks)
                    first = pl.multiple_of(slot * 512, 512)
                    rows = pl.ds(first + i_to * 64 + j_to * 8, 8 * len(js))
                    sums[rows, :] = sums[rows, :] + part


def outer_gradient_kernel(blocks, spot, listed, stacked, grads, own, to_partner, to_across, sums, wide):
    sums[...] = jnp.zeros_like(sums)
    add_gradients(spot, listed, (0, blocks - 1), blocks, stacked, grads, sums, wide)
    own[...] = sums[0 : blocks * 512, :]
    for slot, rim in ((blocks, to_partner), (blocks + 1, to_across)):
        rim[...] = sums[slot * 512 : (slot + 1) * 512, :].T.astype(BF16)


def inner_gradient_kernel(blocks, spot, listed, stacked, grads, outer, turned, sums, wide):
    sums[0 : blocks * 512, :] = outer[...]
    add_gradients(spot, listed, range(1, blocks - 1), blocks, stacked, grads, sums, wide)
    for slot in range(blocks):
        turned[slot] = sums[slot * 512 : (slot + 1) * 512, :].T


def share_kernel(spot, turned, from_partner, from_across, mine, *rest):
    sends, total = rest[:-1], rest[-1]
    blocks, count, share = turned.shape[0], len(sends) + 1, mine.shape[1]
    is_even = spot[1] == 1
    partner, across = from_partner[...].astype(F32), from_across[...].astype(F32)
    total[...] = turned[...]
    total[0] += jnp.where(is_even, across, partner)
    total[blocks - 1] += jnp.where(is_even, partner, across)
    for shift in range(count):
        row = pl.multiple_of(lax.rem(spot[2] + shift, count) * share, share)
        piece = total[:, pl.ds(row, share), :]
        if shift == 0:
            mine[...] = piece
        else:
            sends[shift - 1][...] = piece.astype(BF16)


def shape(*dims, dtype=BF16):
    return jax.ShapeDtypeStruct(dims, dtype)


def call_rims(spot, gathered, occupancy):
    rim = shape(128, 512)
    return pl.pallas_call(
        rim_kernel,
        out_shape=[rim, rim],
        in_specs=[SMEM, VMEM, VMEM],
        out_specs=[VMEM] * 2,
        compiler_params=PARAMS,
        cost_estimate=pl.CostEstimate(flops=10**6, bytes_accessed=10**6, transcendentals=0),
    )(spot, gathered, occupancy)


def scratch_of(blocks, count):
    return [
        pltpu.VMEM(((blocks + 3) * 512, 128), F32),
        pltpu.VMEM((count * CUBE, 128), F32),
        pltpu.VMEM((count * WIDE, 1152), BF16),
    ]


def call_inner(spot, listed, gathered, weight, cotangent, occupancy):
    blocks, out = cotangent.shape[:2]
    return pl.pallas_call(
        inner_kernel,
        out_shape=[
            shape(blocks - 2, out, 512),
            shape(3 * out, 1152),
            shape(3 * out, (blocks - 2) * WIDE),
            shape(3 * out, 1152, dtype=F32),
        ],
        in_specs=[SMEM] * 2 + [VMEM] * 4,
        out_specs=[VMEM] * 4,
        scratch_shapes=scratch_of(blocks, blocks - 2),
        compiler_params=PARAMS,
        cost_estimate=pl.CostEstimate(flops=10**9, bytes_accessed=4 * 10**6, transcendentals=10**5),
    )(spot, listed, gathered, weight, cotangent, occupancy)


def call_outer(spot, listed, gathered, rims, cotangent, occupancy, inner, stacked, product, tiles):
    blocks, out = cotangent.shape[:2]
    return pl.pallas_call(
        outer_kernel,
        out_shape=[
            shape(blocks, out, 512),
            shape(3 * out, 2 * WIDE),
            shape(tiles, 16, 128),
        ],
        in_specs=[SMEM] * 2 + [VMEM] * 8,
        out_specs=[VMEM] * 3,
        scratch_shapes=scratch_of(blocks, 2),
        compiler_params=PARAMS,
        cost_estimate=pl.CostEstimate(flops=10**9, bytes_accessed=4 * 10**6, transcendentals=10**5),
    )(spot, listed, gathered, *rims, cotangent, occupancy, inner, stacked, product)


def call_outer_gradient(spot, listed, stacked, grads):
    blocks = listed.shape[0]
    rim = shape(128, 512)
    return pl.pallas_call(
        functools.partial(outer_gradient_kernel, blocks),
        out_shape=[shape(blocks * 512, 128, dtype=F32), rim, rim],
        in_specs=[SMEM, SMEM, VMEM, VMEM],
        out_specs=[VMEM] * 3,
        scratch_shapes=[
            pltpu.VMEM(((blocks + 3) * 512, 128), F32),
            pltpu.VMEM((WIDE, 1152), F32),
        ],
        compiler_params=PARAMS,
        cost_estimate=pl.CostEstimate(flops=10**9, bytes_accessed=8 * 10**6, transcendentals=0),
    )(spot, listed, stacked, grads)


def call_inner_gradient(spot, listed, stacked, grads, outer):
    blocks = listed.shape[0]
    return pl.pallas_call(
        functools.partial(inner_gradient_kernel, blocks),
        out_shape=shape(blocks, 128, 512, dtype=F32),
        in_specs=[SMEM, SMEM, VMEM, VMEM, VMEM],
        out_specs=VMEM,
        scratch_shapes=[
            pltpu.VMEM(((blocks + 3) * 512, 128), F32),
            pltpu.VMEM((WIDE, 1152), F32),
        ],
        compiler_params=PARAMS,
        cost_estimate=pl.CostEstimate(flops=10**9, bytes_accessed=8 * 10**6, transcendentals=0),
    )(spot, listed, stacked, grads, outer)


def call_share(spot, turned, rims, chan):
    piece = (turned.shape[0], 128 // chan, 512)
    return pl.pallas_call(
        share_kernel,
        out_shape=[shape(*piece, dtype=F32)] + [shape(*piece)] * (chan - 1),
        in_specs=[SMEM] + [VMEM] * 3,
        out_specs=[VMEM] * chan,
        scratch_shapes=[pltpu.VMEM(turned.shape, F32)],
        compiler_params=PARAMS,
        cost_estimate=pl.CostEstimate(flops=10**7, bytes_accessed=4 * 10**6, transcendentals=0),
    )(spot, turned, *rims)


def add_kernel(copies, pieces, out):
    total = pieces[0].astype(F32)
    for n in range(1, pieces.shape[0]):
        total = total + pieces[n].astype(F32)
    for n in range(copies):
        out[n] = total.astype(BF16)


def call_add(pieces, copies):
    return pl.pallas_call(
        functools.partial(add_kernel, copies),
        out_shape=shape(copies, *pieces.shape[1:]),
        in_specs=[VMEM],
        out_specs=VMEM,
        compiler_params=PARAMS,
    )(pieces)


def final_kernel(occupancy, mine, *refs):
    arrived, out = refs[:-1], refs[-1]
    for slot in range(out.shape[0]):
        total = mine[slot]
        for ref in arrived:
            total = total + ref[slot].astype(F32)
        out[slot] = (total * occupancy[slot : slot + 1, :].astype(F32)).astype(BF16)


def call_final(occupancy, mine, arrived):
    return pl.pallas_call(
        final_kernel,
        out_shape=shape(*mine.shape),
        in_specs=[VMEM] * (2 + len(arrived)),
        out_specs=VMEM,
        compiler_params=PARAMS,
    )(occupancy, mine, *arrived)


def stages_of(count):
    return {128: (4, 16, 2), 4: (2, 1, 2), 8: (2, 2, 2), 16: (2, 4, 2)}[count]


def exchange(pieces, groups):
    return lax.all_to_all(pieces, "space", 0, 0, axis_index_groups=groups)


def groups_of(space):
    columns, rows, cores = stages_of(space)
    near, far = {}, {}
    for index in range(space):
        y, z, core = index // (rows * cores), index // cores % rows, index % cores
        near.setdefault(z // 2, []).append(index)
        far.setdefault((y, core, z % 2), []).append(index)
    return list(near.values()), list(far.values())


def on_device(features, occupancy, weight, cotangent, neighbours):
    blocks = features.shape[0]
    out = weight.shape[0]
    space = lax.axis_size("space")
    chan = lax.axis_size("chan")
    near, far = groups_of(space)
    share = -(-108 // len(near[0]))
    place = lax.axis_index("space")

    partner = [(i, i ^ 1) for i in range(space)]
    across = [(i, i - 1 if i % 2 == 0 else i + 1) for i in range(1, space - 1)]
    spot = jnp.stack([place, (place + 1) % 2, lax.axis_index("chan")]).astype(jnp.int32)
    gathered = lax.all_gather(features, "chan", axis=0)
    rims = [
        lax.ppermute(rim, "space", pairs)
        for rim, pairs in zip(call_rims(spot, gathered, occupancy), (partner, across))
    ]

    inner, stacked, inner_grads, product = call_inner(
        spot, neighbours, gathered, jnp.transpose(weight, (1, 0, 2)), cotangent, occupancy
    )
    activation, outer_grads, tiles = call_outer(
        spot, neighbours, gathered, rims, cotangent, occupancy, inner, stacked, product,
        len(near[0]) * share,
    )

    parts = exchange(tiles.reshape(len(near[0]), share, 16, 128), near)
    own, *rims = call_outer_gradient(spot, neighbours, stacked, outer_grads)
    rims = [lax.ppermute(rim, "space", pairs) for rim, pairs in zip(rims, (partner, across))]
    turned = call_inner_gradient(spot, neighbours, stacked, inner_grads, own)
    parts, turned, rims = lax.optimization_barrier((parts, turned, rims))
    parts = exchange(call_add(parts, len(far[0])), far)
    mine, *sends = call_share(spot, turned, rims, chan)
    arrived = [
        lax.ppermute(piece, "chan", [(c, (c + shift + 1) % chan) for c in range(chan)])
        for shift, piece in enumerate(sends)
    ]
    parts, arrived[0], arrived[2] = lax.optimization_barrier((parts, arrived[0], arrived[2]))
    total = exchange(call_add(parts, len(near[0])), near)
    input_grad = call_final(occupancy, mine, arrived)
    total = total.reshape(-1, 16, 128)[:108].astype(F32).reshape(27, out, 128)
    weight_grad = jnp.transpose(total * lax.rsqrt(F32(space * blocks * 512)), (1, 0, 2))

    return (activation, input_grad, weight_grad)


def solution(mesh):
    placed = (
        P("space", "chan", None),
        P("space", None),
        P("chan", None, None),
        P("space", "chan", None),
        P("space", None),
    )
    return jax.shard_map(
        on_device,
        mesh=mesh,
        in_specs=placed,
        out_specs=(P("space", "chan", None), P("space", "chan", None), P("chan", None, None)),
        check_vma=False,
    )
```

```python
import functools

import jax
import jax.numpy as jnp
from jax import lax
from jax.experimental import pallas as pl
from jax.experimental.pallas import tpu as pltpu
from jax.sharding import PartitionSpec as P

F32 = jnp.float32
BF16 = jnp.bfloat16
OFFSETS = [(a, b, c) for a in (-1, 0, 1) for b in (-1, 0, 1) for c in (-1, 0, 1)]
NT = (((1,), (1,)), ((), ()))
CUBE = 1616
WIDE = 640
FLIPS = (2, 1, 3)
VMEM = pl.BlockSpec(memory_space=pltpu.VMEM)
SMEM = pl.BlockSpec(memory_space=pltpu.SMEM)
PARAMS = pltpu.CompilerParams(vmem_limit_bytes=24 * 1024 * 1024)
SMALL = pltpu.CompilerParams(vmem_limit_bytes=8 * 1024 * 1024)


def spans(shift):
    if shift < 0:
        return [(0, 7)]
    if shift > 0:
        return [(9, 0)]
    return [(1 + i, i) for i in range(8)]


def slot_of(spot, listed, block, number, blocks):
    if number == 13:
        return block
    name = listed[block, number if number < 13 else number - 1]
    local = name - spot[0] * blocks
    is_even = lax.rem(spot[0], 2) == 0
    below = jnp.where(is_even, blocks + 1, blocks)
    above = jnp.where(is_even, blocks, blocks + 1)
    local = jnp.where(local == -1, below, jnp.where(local == blocks, above, local))
    return jnp.where(name < 0, blocks + 2, local)


def fill_cube(spot, listed, block, blocks, voxels, cube, base):
    for number, (a, b, c) in enumerate(OFFSETS):
        first = pl.multiple_of(slot_of(spot, listed, block, number, blocks) * 512, 512)
        for i_to, i_from in spans(a):
            if c == 0:
                for j_to, j_from in spans(b):
                    row = base + (i_to * 10 + j_to) * 16 + 8
                    cube[row : row + 8, :] = voxels[pl.ds(first + i_from * 64 + j_from * 8, 8), :]
                continue
            k_from, k_to = (7, 7) if c < 0 else (0, 16)
            if b == 0:
                source = pl.ds(first + i_from * 64 + k_from, 8, stride=8)
                cube[pl.ds(base + (i_to * 10 + 1) * 16 + k_to, 8, stride=16), :] = voxels[source, :]
            else:
                ((j_to, j_from),) = spans(b)
                row = base + (i_to * 10 + j_to) * 16 + k_to
                source = pl.ds(first + i_from * 64 + j_from * 8 + k_from, 1)
                cube[row : row + 1, :] = voxels[source, :]


def pack_patches(cube, base, patches, top):
    for i in range(10):
        for c in range(3):
            rows = [
                cube[base + (i * 10 + j) * 16 + 7 + c : base + (i * 10 + j) * 16 + 15 + c, :]
                for j in range(10)
            ]
            pairs = [
                jnp.concatenate([rows[j], rows[j + 1]], axis=0).astype(BF16) for j in range(9)
            ]
            for b in range(3):
                lanes = (3 * b + c) * 128
                for t in range(4):
                    row = top + i * 64 + t * 16
                    patches[row : row + 16, lanes : lanes + 128] = pairs[2 * t + b]


def load_block(gathered, occupancy, slot):
    block = jnp.concatenate([gathered[c, slot] for c in range(gathered.shape[0])], axis=0)
    return block.astype(F32) * occupancy[slot : slot + 1, :].astype(F32)


def rim_kernel(spot, gathered, occupancy, to_partner, to_across):
    first = load_block(gathered, occupancy, 0).astype(BF16)
    last = load_block(gathered, occupancy, gathered.shape[1] - 1).astype(BF16)
    is_even = lax.rem(spot[0], 2) == 0
    to_partner[...] = jnp.where(is_even, last, first)
    to_across[...] = jnp.where(is_even, first, last)


def forward_block(
    spot, listed, block, stacked, cotangent, occupancy, voxels, cube, patches, grads, place
):
    base, top = place * CUBE, place * WIDE
    fill_cube(spot, listed, block, cotangent.shape[0], voxels, cube, base)
    pack_patches(cube, base, patches, top)
    wide = lax.dot_general(
        stacked[...], patches[top : top + WIDE, :], NT, preferred_element_type=F32
    )
    pre = (
        wide[0:64, 0:512]
        + pltpu.roll(wide[64:128], WIDE - 64, 1)[:, 0:512]
        + wide[128:192, 128:640]
    )
    live = occupancy[block : block + 1, :].astype(F32)
    sigma = jax.nn.sigmoid(pre)
    slope = sigma * (1.0 + pre * (1.0 - sigma))
    grad = (cotangent[block].astype(F32) * slope * live).astype(BF16).astype(F32)
    grad = jnp.concatenate([grad, jnp.zeros((64, 128), F32)], axis=1)
    lanes = slice(top, top + WIDE)
    grads[0:64, lanes] = grad.astype(BF16)
    grads[64:128, lanes] = pltpu.roll(grad, 64, 1).astype(BF16)
    grads[128:192, lanes] = pltpu.roll(grad, 128, 1).astype(BF16)
    return (pre * sigma * live).astype(BF16)


def own_voxels(gathered, occupancy, voxels):
    blocks = gathered.shape[1]
    for slot in range(blocks):
        block = load_block(gathered, occupancy, slot)
        voxels[slot * 512 : (slot + 1) * 512, :] = block.T
    voxels[(blocks + 2) * 512 : (blocks + 3) * 512, :] = jnp.zeros((512, 128), F32)


def inner_kernel(
    spot, listed, gathered, weight, cotangent, occupancy,
    activation, stacked, grads, product, own,
    voxels, cube, patches,
):
    blocks = cotangent.shape[0]
    out = weight.shape[1]
    for number in range(27):
        a, lanes = number // 9, number % 9 * 128
        stacked[a * out : (a + 1) * out, lanes : lanes + 128] = weight[number]
    own_voxels(gathered, occupancy, voxels)
    own[...] = voxels[0 : blocks * 512, :]
    for block in range(1, blocks - 1):
        activation[block - 1] = forward_block(
            spot, listed, block, stacked, cotangent, occupancy, voxels, cube, patches, grads,
            block - 1,
        )
    for first in range(0, 9, 2):
        lanes = slice(first * 128, min(first + 2, 9) * 128)
        product[:, lanes] = jnp.dot(grads[...], patches[:, lanes], preferred_element_type=F32)


def outer_kernel(
    spot, listed, own, from_partner, from_across, cotangent, occupancy, inner, stacked, product,
    activation, grads, tiles,
    voxels, cube, patches,
):
    blocks = cotangent.shape[0]
    voxels[0 : blocks * 512, :] = own[...]
    voxels[(blocks + 2) * 512 : (blocks + 3) * 512, :] = jnp.zeros((512, 128), F32)
    for slot, rim in ((blocks, from_partner), (blocks + 1, from_across)):
        voxels[slot * 512 : (slot + 1) * 512, :] = rim[...].astype(F32).T
    activation[1 : blocks - 1] = inner[...]
    for place, block in enumerate((0, blocks - 1)):
        activation[block] = forward_block(
            spot, listed, block, stacked, cotangent, occupancy, voxels, cube, patches, grads, place
        )
    for first in range(0, 9, 2):
        count = min(2, 9 - first)
        lanes = slice(first * 128, (first + count) * 128)
        part = product[:, lanes] + jnp.dot(
            grads[...], patches[:, lanes], preferred_element_type=F32
        )
        for t in range(count):
            for r in range(12):
                corner = part[r * 16 : (r + 1) * 16, t * 128 : (t + 1) * 128]
                tiles[(r // 4 * 9 + first + t) * 4 + r % 4] = corner.astype(BF16)
    for t in range(108, tiles.shape[0]):
        tiles[t] = jnp.zeros((16, 128), BF16)


def add_gradients(spot, listed, picked, blocks, stacked, grads, sums, wide):
    edge = lax.broadcasted_iota(jnp.int32, (8, 128), 0)
    for at, p in enumerate(picked):
        turn = grads[:, at * WIDE : (at + 1) * WIDE].astype(F32).T.astype(BF16)
        wide[...] = jnp.dot(turn, stacked[...], preferred_element_type=F32)
        for i in range(10):
            a, i_to = (-1, 7) if i == 0 else ((1, 0) if i == 9 else (0, i - 1))

            def line(j, c):
                total = None
                for b in range(3):
                    if 0 <= j - b < 8:
                        row = i * 64 + (j - b) * 8
                        lanes = (3 * b + c) * 128
                        term = wide[row : row + 8, lanes : lanes + 128]
                        total = term if total is None else total + term
                return total

            for b, js in ((-1, [0]), (0, list(range(1, 9))), (1, [9])):
                before = [pltpu.roll(line(j, 0), 7, 0) for j in js]
                centre = [line(j, 1) for j in js]
                after = [pltpu.roll(line(j, 2), 1, 0) for j in js]
                j_to = 7 if b < 0 else 0
                for c in (-1, 0, 1):
                    if c < 0:
                        parts = [jnp.where(edge == 7, x, 0.0) for x in before]
                    elif c > 0:
                        parts = [jnp.where(edge == 0, x, 0.0) for x in after]
                    else:
                        parts = [
                            y + jnp.where(edge < 7, x, 0.0) + jnp.where(edge > 0, z, 0.0)
                            for x, y, z in zip(before, centre, after)
                        ]
                    part = parts[0] if len(parts) == 1 else jnp.concatenate(parts, axis=0)
                    number = 9 * (a + 1) + 3 * (b + 1) + c + 1
                    slot = slot_of(spot, listed, p, number, blocks)
                    first = pl.multiple_of(slot * 512, 512)
                    rows = pl.ds(first + i_to * 64 + j_to * 8, 8 * len(js))
                    sums[rows, :] = sums[rows, :] + part


def backward_kernel(
    blocks, spot, ring_spot, listed, stacked, inner, outer, mine, *rest
):
    sends, (sums, wide, turned) = rest[:-3], rest[-3:]
    sums[...] = jnp.zeros_like(sums)
    add_gradients(spot, listed, (0, blocks - 1), blocks, stacked, outer, sums, wide)
    add_gradients(spot, listed, range(1, blocks - 1), blocks, stacked, inner, sums, wide)
    share = mine.shape[1]
    for slot in range(blocks + 2):
        turned[slot * 128 : (slot + 1) * 128, :] = sums[slot * 512 : (slot + 1) * 512, :].T
    for flip, ref in zip((0,) + FLIPS, (mine,) + tuple(sends)):
        row = pl.multiple_of((ring_spot[0] ^ flip) * share, share)
        for slot in range(blocks + 2):
            ref[slot] = turned[pl.ds(slot * 128 + row, share), :].astype(ref.dtype)


def shape(*dims, dtype=BF16):
    return jax.ShapeDtypeStruct(dims, dtype)


def call_rims(spot, gathered, occupancy):
    rim = shape(128, 512)
    return pl.pallas_call(
        rim_kernel,
        out_shape=[rim, rim],
        in_specs=[SMEM, VMEM, VMEM],
        out_specs=[VMEM] * 2,
        compiler_params=SMALL,
        cost_estimate=pl.CostEstimate(flops=10**6, bytes_accessed=10**6, transcendentals=0),
    )(spot, gathered, occupancy)


def scratch_of(blocks, count):
    return [
        pltpu.VMEM(((blocks + 3) * 512, 128), F32),
        pltpu.VMEM((count * CUBE, 128), F32),
        pltpu.VMEM((count * WIDE, 1152), BF16),
    ]


def call_inner(spot, listed, gathered, weight, cotangent, occupancy):
    blocks, out = cotangent.shape[:2]
    return pl.pallas_call(
        inner_kernel,
        out_shape=[
            shape(blocks - 2, out, 512),
            shape(3 * out, 1152),
            shape(3 * out, (blocks - 2) * WIDE),
            shape(3 * out, 1152, dtype=F32),
            shape(blocks * 512, 128, dtype=F32),
        ],
        in_specs=[SMEM] * 2 + [VMEM] * 4,
        out_specs=[VMEM] * 5,
        scratch_shapes=scratch_of(blocks, blocks - 2),
        compiler_params=PARAMS,
        cost_estimate=pl.CostEstimate(flops=10**9, bytes_accessed=4 * 10**6, transcendentals=10**5),
    )(spot, listed, gathered, weight, cotangent, occupancy)


def call_outer(spot, listed, own, rims, cotangent, occupancy, inner, stacked, product, tiles):
    blocks, out = cotangent.shape[:2]
    return pl.pallas_call(
        outer_kernel,
        out_shape=[
            shape(blocks, out, 512),
            shape(3 * out, 2 * WIDE),
            shape(tiles, 16, 128),
        ],
        in_specs=[SMEM] * 2 + [VMEM] * 8,
        out_specs=[VMEM] * 3,
        scratch_shapes=scratch_of(blocks, 2),
        compiler_params=PARAMS,
        cost_estimate=pl.CostEstimate(flops=10**9, bytes_accessed=4 * 10**6, transcendentals=10**5),
    )(spot, listed, own, *rims, cotangent, occupancy, inner, stacked, product)


def call_backward(spot, ring_spot, listed, stacked, inner, outer, chan):
    blocks = listed.shape[0]
    piece = (blocks + 2, 128 // chan, 512)
    return pl.pallas_call(
        functools.partial(backward_kernel, blocks),
        out_shape=[shape(*piece, dtype=F32)] + [shape(*piece)] * (chan - 1),
        in_specs=[SMEM] * 3 + [VMEM] * 3,
        out_specs=[VMEM] * chan,
        scratch_shapes=[
            pltpu.VMEM(((blocks + 3) * 512, 128), F32),
            pltpu.VMEM((WIDE, 1152), F32),
            pltpu.VMEM(((blocks + 2) * 128, 512), F32),
        ],
        compiler_params=PARAMS,
        cost_estimate=pl.CostEstimate(flops=2 * 10**9, bytes_accessed=8 * 10**6, transcendentals=0),
    )(spot, ring_spot, listed, stacked, inner, outer)


def add_kernel(copies, pieces, out):
    total = pieces[0].astype(F32)
    for n in range(1, pieces.shape[0]):
        total = total + pieces[n].astype(F32)
    for n in range(copies):
        out[n] = total.astype(BF16)


def call_add(pieces, copies):
    return pl.pallas_call(
        functools.partial(add_kernel, copies),
        out_shape=shape(copies, *pieces.shape[1:]),
        in_specs=[VMEM],
        out_specs=VMEM,
        compiler_params=SMALL,
    )(pieces)


def sum_kernel(blocks, mine, *refs):
    arrived, (own, to_partner, to_across) = refs[:-3], refs[-3:]
    for slot in range(blocks + 2):
        total = mine[slot]
        for ref in arrived:
            total = total + ref[slot].astype(F32)
        if slot < blocks:
            own[slot] = total
        else:
            (to_partner if slot == blocks else to_across)[...] = total.astype(BF16)


def call_sum(mine, arrived):
    blocks, rim = mine.shape[0] - 2, mine.shape[1:]
    return pl.pallas_call(
        functools.partial(sum_kernel, blocks),
        out_shape=[shape(blocks, *rim, dtype=F32), shape(*rim), shape(*rim)],
        in_specs=[VMEM] * (1 + len(arrived)),
        out_specs=[VMEM] * 3,
        compiler_params=SMALL,
    )(mine, *arrived)


def final_kernel(spot, own, from_partner, from_across, occupancy, out):
    blocks = own.shape[0]
    is_even = lax.rem(spot[0], 2) == 0
    partner, across = from_partner[...].astype(F32), from_across[...].astype(F32)
    for slot in range(blocks):
        total = own[slot]
        if slot == 0:
            total = total + jnp.where(is_even, across, partner)
        if slot == blocks - 1:
            total = total + jnp.where(is_even, partner, across)
        out[slot] = (total * occupancy[slot : slot + 1, :].astype(F32)).astype(BF16)


def call_final(spot, own, from_partner, from_across, occupancy):
    return pl.pallas_call(
        final_kernel,
        out_shape=shape(*own.shape),
        in_specs=[SMEM] + [VMEM] * 4,
        out_specs=VMEM,
        compiler_params=SMALL,
    )(spot, own, from_partner, from_across, occupancy)


def stages_of(count):
    return {128: (4, 16, 2), 4: (2, 1, 2), 8: (2, 2, 2), 16: (2, 4, 2)}[count]


def exchange(pieces, groups):
    return lax.all_to_all(pieces, "space", 0, 0, axis_index_groups=groups)


def groups_of(space):
    columns, rows, cores = stages_of(space)
    near, far = {}, {}
    for index in range(space):
        y, z, core = index // (rows * cores), index // cores % rows, index % cores
        near.setdefault(z // 2, []).append(index)
        far.setdefault((y, core, z % 2), []).append(index)
    return list(near.values()), list(far.values())


def on_device(features, occupancy, weight, cotangent, neighbours):
    blocks = features.shape[0]
    out = weight.shape[0]
    space = lax.axis_size("space")
    chan = lax.axis_size("chan")
    near, far = groups_of(space)
    share = -(-108 // len(near[0]))
    place = lax.axis_index("space")

    partner = [(i, i ^ 1) for i in range(space)]
    across = [(i, i - 1 if i % 2 == 0 else i + 1) for i in range(1, space - 1)]
    spot = place.astype(jnp.int32).reshape(1)
    ring_spot = lax.axis_index("chan").astype(jnp.int32).reshape(1)
    gathered = lax.all_to_all(
        jnp.broadcast_to(features, (chan,) + features.shape), "chan", 0, 0
    )
    rims = [
        lax.ppermute(rim, "space", pairs)
        for rim, pairs in zip(call_rims(spot, gathered, occupancy), (partner, across))
    ]

    inner, stacked, inner_grads, product, own = call_inner(
        spot, neighbours, gathered, jnp.transpose(weight, (1, 0, 2)), cotangent, occupancy
    )
    activation, outer_grads, tiles = call_outer(
        spot, neighbours, own, rims, cotangent, occupancy, inner, stacked, product,
        len(near[0]) * share,
    )

    parts = exchange(tiles.reshape(len(near[0]), share, 16, 128), near)
    mine, *sends = call_backward(
        spot, ring_spot, neighbours, stacked, inner_grads, outer_grads, chan
    )
    parts, mine, sends = lax.optimization_barrier((parts, mine, sends))
    parts = exchange(call_add(parts, len(far[0])), far)
    arrived = [
        lax.ppermute(piece, "chan", [(c, c ^ flip) for c in range(chan)])
        for flip, piece in zip(FLIPS, sends)
    ]
    parts, arrived = lax.optimization_barrier((parts, arrived))
    total = exchange(call_add(parts, len(near[0])), near)
    own, rim_partner, rim_across = call_sum(mine, arrived)
    to_partner = lax.ppermute(rim_partner, "space", partner)
    to_across = lax.ppermute(rim_across, "space", across)
    total = total.reshape(-1, 16, 128)[:108].astype(F32).reshape(27, out, 128)
    weight_grad = jnp.transpose(total * lax.rsqrt(F32(space * blocks * 512)), (1, 0, 2))

    input_grad = call_final(spot, own, to_partner, to_across, occupancy)
    return (activation, input_grad, weight_grad)


def solution(mesh):
    placed = (
        P("space", "chan", None),
        P("space", None),
        P("chan", None, None),
        P("space", "chan", None),
        P("space", None),
    )
    return jax.shard_map(
        on_device,
        mesh=mesh,
        in_specs=placed,
        out_specs=(P("space", "chan", None), P("space", "chan", None), P("chan", None, None)),
        check_vma=False,
    )
```

```python
import functools

import jax
import jax.numpy as jnp
from jax import lax
from jax.experimental import pallas as pl
from jax.experimental.pallas import tpu as pltpu
from jax.sharding import PartitionSpec as P

F32 = jnp.float32
BF16 = jnp.bfloat16
OFFSETS = [(a, b, c) for a in (-1, 0, 1) for b in (-1, 0, 1) for c in (-1, 0, 1)]
NT = (((1,), (1,)), ((), ()))
CUBE = 1616
WIDE = 640
FLIPS = (2, 1, 3)
VMEM = pl.BlockSpec(memory_space=pltpu.VMEM)
SMEM = pl.BlockSpec(memory_space=pltpu.SMEM)
PARAMS = pltpu.CompilerParams(vmem_limit_bytes=24 * 1024 * 1024)
SMALL = pltpu.CompilerParams(vmem_limit_bytes=8 * 1024 * 1024)


def spans(shift):
    if shift < 0:
        return [(0, 7)]
    if shift > 0:
        return [(9, 0)]
    return [(1 + i, i) for i in range(8)]


def slot_of(spot, listed, block, number, blocks):
    if number == 13:
        return block
    name = listed[block, number if number < 13 else number - 1]
    local = name - spot[0] * blocks
    is_even = lax.rem(spot[0], 2) == 0
    below = jnp.where(is_even, blocks + 1, blocks)
    above = jnp.where(is_even, blocks, blocks + 1)
    local = jnp.where(local == -1, below, jnp.where(local == blocks, above, local))
    return jnp.where(name < 0, blocks + 2, local)


def fill_cube(spot, listed, block, blocks, voxels, cube, base):
    for number, (a, b, c) in enumerate(OFFSETS):
        first = pl.multiple_of(slot_of(spot, listed, block, number, blocks) * 512, 512)
        for i_to, i_from in spans(a):
            if c == 0:
                for j_to, j_from in spans(b):
                    row = base + (i_to * 10 + j_to) * 16 + 8
                    cube[row : row + 8, :] = voxels[pl.ds(first + i_from * 64 + j_from * 8, 8), :]
                continue
            k_from, k_to = (7, 7) if c < 0 else (0, 16)
            if b == 0:
                source = pl.ds(first + i_from * 64 + k_from, 8, stride=8)
                cube[pl.ds(base + (i_to * 10 + 1) * 16 + k_to, 8, stride=16), :] = voxels[source, :]
            else:
                ((j_to, j_from),) = spans(b)
                row = base + (i_to * 10 + j_to) * 16 + k_to
                source = pl.ds(first + i_from * 64 + j_from * 8 + k_from, 1)
                cube[row : row + 1, :] = voxels[source, :]


def pack_patches(cube, base, patches, top):
    for i in range(10):
        for c in range(3):
            rows = [
                cube[base + (i * 10 + j) * 16 + 7 + c : base + (i * 10 + j) * 16 + 15 + c, :]
                for j in range(10)
            ]
            pairs = [
                jnp.concatenate([rows[j], rows[j + 1]], axis=0).astype(BF16) for j in range(9)
            ]
            for b in range(3):
                lanes = (3 * b + c) * 128
                for t in range(4):
                    row = top + i * 64 + t * 16
                    patches[row : row + 16, lanes : lanes + 128] = pairs[2 * t + b]


def load_block(gathered, occupancy, slot):
    block = jnp.concatenate([gathered[c, slot] for c in range(gathered.shape[0])], axis=0)
    return block.astype(F32) * occupancy[slot : slot + 1, :].astype(F32)


def rim_kernel(spot, gathered, occupancy, to_partner, to_across):
    first = load_block(gathered, occupancy, 0).astype(BF16)
    last = load_block(gathered, occupancy, gathered.shape[1] - 1).astype(BF16)
    is_even = lax.rem(spot[0], 2) == 0
    to_partner[...] = jnp.where(is_even, last, first)
    to_across[...] = jnp.where(is_even, first, last)


def forward_block(
    spot, listed, block, stacked, cotangent, occupancy, voxels, cube, patches, grads, place
):
    base, top = place * CUBE, place * WIDE
    fill_cube(spot, listed, block, cotangent.shape[0], voxels, cube, base)
    pack_patches(cube, base, patches, top)
    wide = lax.dot_general(
        stacked[...], patches[top : top + WIDE, :], NT, preferred_element_type=F32
    )
    pre = (
        wide[0:64, 0:512]
        + pltpu.roll(wide[64:128], WIDE - 64, 1)[:, 0:512]
        + wide[128:192, 128:640]
    )
    live = occupancy[block : block + 1, :].astype(F32)
    sigma = jax.nn.sigmoid(pre)
    slope = sigma * (1.0 + pre * (1.0 - sigma))
    grad = (cotangent[block].astype(F32) * slope * live).astype(BF16).astype(F32)
    grad = jnp.concatenate([grad, jnp.zeros((64, 128), F32)], axis=1)
    lanes = slice(top, top + WIDE)
    grads[0:64, lanes] = grad.astype(BF16)
    grads[64:128, lanes] = pltpu.roll(grad, 64, 1).astype(BF16)
    grads[128:192, lanes] = pltpu.roll(grad, 128, 1).astype(BF16)
    return (pre * sigma * live).astype(BF16)


def own_voxels(gathered, occupancy, voxels):
    blocks = gathered.shape[1]
    for slot in range(blocks):
        block = load_block(gathered, occupancy, slot)
        voxels[slot * 512 : (slot + 1) * 512, :] = block.T
    voxels[(blocks + 2) * 512 : (blocks + 3) * 512, :] = jnp.zeros((512, 128), F32)


def inner_kernel(
    spot, listed, gathered, weight, cotangent, occupancy,
    activation, stacked, grads, product, own,
    voxels, cube, patches,
):
    blocks = cotangent.shape[0]
    out = weight.shape[1]
    for number in range(27):
        a, lanes = number // 9, number % 9 * 128
        stacked[a * out : (a + 1) * out, lanes : lanes + 128] = weight[number]
    own_voxels(gathered, occupancy, voxels)
    own[...] = voxels[0 : blocks * 512, :]
    for block in range(1, blocks - 1):
        activation[block - 1] = forward_block(
            spot, listed, block, stacked, cotangent, occupancy, voxels, cube, patches, grads,
            block - 1,
        )
    for first in range(0, 9, 2):
        lanes = slice(first * 128, min(first + 2, 9) * 128)
        product[:, lanes] = jnp.dot(grads[...], patches[:, lanes], preferred_element_type=F32)


def outer_kernel(
    spot, listed, own, from_partner, from_across, cotangent, occupancy, inner, stacked, product,
    activation, grads, tiles,
    voxels, cube, patches,
):
    blocks = cotangent.shape[0]
    voxels[0 : blocks * 512, :] = own[...]
    voxels[(blocks + 2) * 512 : (blocks + 3) * 512, :] = jnp.zeros((512, 128), F32)
    for slot, rim in ((blocks, from_partner), (blocks + 1, from_across)):
        voxels[slot * 512 : (slot + 1) * 512, :] = rim[...].astype(F32).T
    activation[1 : blocks - 1] = inner[...]
    for place, block in enumerate((0, blocks - 1)):
        activation[block] = forward_block(
            spot, listed, block, stacked, cotangent, occupancy, voxels, cube, patches, grads, place
        )
    for first in range(0, 9, 2):
        count = min(2, 9 - first)
        lanes = slice(first * 128, (first + count) * 128)
        part = product[:, lanes] + jnp.dot(
            grads[...], patches[:, lanes], preferred_element_type=F32
        )
        for t in range(count):
            for r in range(12):
                corner = part[r * 16 : (r + 1) * 16, t * 128 : (t + 1) * 128]
                tiles[(r // 4 * 9 + first + t) * 4 + r % 4] = corner.astype(BF16)
    for t in range(108, tiles.shape[0]):
        tiles[t] = jnp.zeros((16, 128), BF16)


def add_gradients(spot, listed, picked, blocks, stacked, grads, sums, wide):
    edge = lax.broadcasted_iota(jnp.int32, (8, 128), 0)
    for at, p in enumerate(picked):
        turn = grads[:, at * WIDE : (at + 1) * WIDE].astype(F32).T.astype(BF16)
        wide[...] = jnp.dot(turn, stacked[...], preferred_element_type=F32)
        for i in range(10):
            a, i_to = (-1, 7) if i == 0 else ((1, 0) if i == 9 else (0, i - 1))

            def line(j, c):
                total = None
                for b in range(3):
                    if 0 <= j - b < 8:
                        row = i * 64 + (j - b) * 8
                        lanes = (3 * b + c) * 128
                        term = wide[row : row + 8, lanes : lanes + 128]
                        total = term if total is None else total + term
                return total

            for b, js in ((-1, [0]), (0, list(range(1, 9))), (1, [9])):
                before = [pltpu.roll(line(j, 0), 7, 0) for j in js]
                centre = [line(j, 1) for j in js]
                after = [pltpu.roll(line(j, 2), 1, 0) for j in js]
                j_to = 7 if b < 0 else 0
                for c in (-1, 0, 1):
                    if c < 0:
                        parts = [jnp.where(edge == 7, x, 0.0) for x in before]
                    elif c > 0:
                        parts = [jnp.where(edge == 0, x, 0.0) for x in after]
                    else:
                        parts = [
                            y + jnp.where(edge < 7, x, 0.0) + jnp.where(edge > 0, z, 0.0)
                            for x, y, z in zip(before, centre, after)
                        ]
                    part = parts[0] if len(parts) == 1 else jnp.concatenate(parts, axis=0)
                    number = 9 * (a + 1) + 3 * (b + 1) + c + 1
                    slot = slot_of(spot, listed, p, number, blocks)
                    first = pl.multiple_of(slot * 512, 512)
                    rows = pl.ds(first + i_to * 64 + j_to * 8, 8 * len(js))
                    sums[rows, :] = sums[rows, :] + part


def backward_kernel(
    blocks, spot, ring_spot, listed, stacked, inner, outer, mine, *rest
):
    sends, (sums, wide, turned) = rest[:-3], rest[-3:]
    sums[...] = jnp.zeros_like(sums)
    add_gradients(spot, listed, (0, blocks - 1), blocks, stacked, outer, sums, wide)
    add_gradients(spot, listed, range(1, blocks - 1), blocks, stacked, inner, sums, wide)
    share = mine.shape[1]
    for slot in range(blocks + 2):
        turned[slot * 128 : (slot + 1) * 128, :] = sums[slot * 512 : (slot + 1) * 512, :].T
    for flip, ref in zip((0,) + FLIPS, (mine,) + tuple(sends)):
        row = pl.multiple_of((ring_spot[0] ^ flip) * share, share)
        for slot in range(blocks + 2):
            ref[slot] = turned[pl.ds(slot * 128 + row, share), :].astype(ref.dtype)


def shape(*dims, dtype=BF16):
    return jax.ShapeDtypeStruct(dims, dtype)


def call_rims(spot, gathered, occupancy):
    rim = shape(128, 512)
    return pl.pallas_call(
        rim_kernel,
        out_shape=[rim, rim],
        in_specs=[SMEM, VMEM, VMEM],
        out_specs=[VMEM] * 2,
        compiler_params=SMALL,
        cost_estimate=pl.CostEstimate(flops=10**6, bytes_accessed=10**6, transcendentals=0),
    )(spot, gathered, occupancy)


def scratch_of(blocks, count):
    return [
        pltpu.VMEM(((blocks + 3) * 512, 128), F32),
        pltpu.VMEM((count * CUBE, 128), F32),
        pltpu.VMEM((count * WIDE, 1152), BF16),
    ]


def call_inner(spot, listed, gathered, weight, cotangent, occupancy):
    blocks, out = cotangent.shape[:2]
    return pl.pallas_call(
        inner_kernel,
        out_shape=[
            shape(blocks - 2, out, 512),
            shape(3 * out, 1152),
            shape(3 * out, (blocks - 2) * WIDE),
            shape(3 * out, 1152, dtype=F32),
            shape(blocks * 512, 128, dtype=F32),
        ],
        in_specs=[SMEM] * 2 + [VMEM] * 4,
        out_specs=[VMEM] * 5,
        scratch_shapes=scratch_of(blocks, blocks - 2),
        compiler_params=PARAMS,
        cost_estimate=pl.CostEstimate(flops=10**9, bytes_accessed=4 * 10**6, transcendentals=10**5),
    )(spot, listed, gathered, weight, cotangent, occupancy)


def call_outer(spot, listed, own, rims, cotangent, occupancy, inner, stacked, product, tiles):
    blocks, out = cotangent.shape[:2]
    return pl.pallas_call(
        outer_kernel,
        out_shape=[
            shape(blocks, out, 512),
            shape(3 * out, 2 * WIDE),
            shape(tiles, 16, 128),
        ],
        in_specs=[SMEM] * 2 + [VMEM] * 8,
        out_specs=[VMEM] * 3,
        scratch_shapes=scratch_of(blocks, 2),
        compiler_params=PARAMS,
        cost_estimate=pl.CostEstimate(flops=10**9, bytes_accessed=4 * 10**6, transcendentals=10**5),
    )(spot, listed, own, *rims, cotangent, occupancy, inner, stacked, product)


def call_backward(spot, ring_spot, listed, stacked, inner, outer, chan):
    blocks = listed.shape[0]
    piece = (blocks + 2, 128 // chan, 512)
    return pl.pallas_call(
        functools.partial(backward_kernel, blocks),
        out_shape=[shape(*piece, dtype=F32)] + [shape(*piece)] * (chan - 1),
        in_specs=[SMEM] * 3 + [VMEM] * 3,
        out_specs=[VMEM] * chan,
        scratch_shapes=[
            pltpu.VMEM(((blocks + 3) * 512, 128), F32),
            pltpu.VMEM((WIDE, 1152), F32),
            pltpu.VMEM(((blocks + 2) * 128, 512), F32),
        ],
        compiler_params=PARAMS,
        cost_estimate=pl.CostEstimate(flops=2 * 10**9, bytes_accessed=8 * 10**6, transcendentals=0),
    )(spot, ring_spot, listed, stacked, inner, outer)


def add_kernel(copies, pieces, out):
    total = pieces[0].astype(F32)
    for n in range(1, pieces.shape[0]):
        total = total + pieces[n].astype(F32)
    for n in range(copies):
        out[n] = total.astype(BF16)


def call_add(pieces, copies):
    return pl.pallas_call(
        functools.partial(add_kernel, copies),
        out_shape=shape(copies, *pieces.shape[1:]),
        in_specs=[VMEM],
        out_specs=VMEM,
        compiler_params=SMALL,
    )(pieces)


def sum_kernel(blocks, mine, *refs):
    arrived, (own, to_partner, to_across) = refs[:-3], refs[-3:]
    for slot in range(blocks + 2):
        total = mine[slot]
        for ref in arrived:
            total = total + ref[slot].astype(F32)
        if slot < blocks:
            own[slot] = total
        else:
            (to_partner if slot == blocks else to_across)[...] = total.astype(BF16)


def call_sum(mine, arrived):
    blocks, rim = mine.shape[0] - 2, mine.shape[1:]
    return pl.pallas_call(
        functools.partial(sum_kernel, blocks),
        out_shape=[shape(blocks, *rim, dtype=F32), shape(*rim), shape(*rim)],
        in_specs=[VMEM] * (1 + len(arrived)),
        out_specs=[VMEM] * 3,
        compiler_params=SMALL,
    )(mine, *arrived)


def final_kernel(spot, own, from_partner, from_across, occupancy, out):
    blocks = own.shape[0]
    is_even = lax.rem(spot[0], 2) == 0
    partner, across = from_partner[...].astype(F32), from_across[...].astype(F32)
    for slot in range(blocks):
        total = own[slot]
        if slot == 0:
            total = total + jnp.where(is_even, across, partner)
        if slot == blocks - 1:
            total = total + jnp.where(is_even, partner, across)
        out[slot] = (total * occupancy[slot : slot + 1, :].astype(F32)).astype(BF16)


def call_final(spot, own, from_partner, from_across, occupancy):
    return pl.pallas_call(
        final_kernel,
        out_shape=shape(*own.shape),
        in_specs=[SMEM] + [VMEM] * 4,
        out_specs=VMEM,
        compiler_params=SMALL,
    )(spot, own, from_partner, from_across, occupancy)


def stages_of(count):
    return {128: (4, 16, 2), 4: (2, 1, 2), 8: (2, 2, 2), 16: (2, 4, 2)}[count]


def exchange(pieces, groups):
    return lax.all_to_all(pieces, "space", 0, 0, axis_index_groups=groups)


def groups_of(space):
    columns, rows, cores = stages_of(space)
    near, far = {}, {}
    for index in range(space):
        y, z, core = index // (rows * cores), index // cores % rows, index % cores
        near.setdefault(z // 2, []).append(index)
        far.setdefault((y, core, z % 2), []).append(index)
    return list(near.values()), list(far.values())


def on_device(features, occupancy, weight, cotangent, neighbours):
    blocks = features.shape[0]
    out = weight.shape[0]
    space = lax.axis_size("space")
    chan = lax.axis_size("chan")
    near, far = groups_of(space)
    share = -(-108 // len(near[0]))
    place = lax.axis_index("space")

    partner = [(i, i ^ 1) for i in range(space)]
    across = [(i, i - 1 if i % 2 == 0 else i + 1) for i in range(1, space - 1)]
    spot = place.astype(jnp.int32).reshape(1)
    ring_spot = lax.axis_index("chan").astype(jnp.int32).reshape(1)
    gathered = lax.all_gather(features, "chan", axis=0)
    rims = [
        lax.ppermute(rim, "space", pairs)
        for rim, pairs in zip(call_rims(spot, gathered, occupancy), (partner, across))
    ]

    inner, stacked, inner_grads, product, own = call_inner(
        spot, neighbours, gathered, jnp.transpose(weight, (1, 0, 2)), cotangent, occupancy
    )
    activation, outer_grads, tiles = call_outer(
        spot, neighbours, own, rims, cotangent, occupancy, inner, stacked, product,
        len(near[0]) * share,
    )

    parts = exchange(tiles.reshape(len(near[0]), share, 16, 128), near)
    mine, *sends = call_backward(
        spot, ring_spot, neighbours, stacked, inner_grads, outer_grads, chan
    )
    parts, mine, sends = lax.optimization_barrier((parts, mine, sends))
    parts = exchange(call_add(parts, len(far[0])), far)
    arrived = [
        lax.ppermute(piece, "chan", [(c, c ^ flip) for c in range(chan)])
        for flip, piece in zip(FLIPS, sends)
    ]
    parts, arrived = lax.optimization_barrier((parts, arrived))
    total = exchange(call_add(parts, len(near[0])), near)
    own, rim_partner, rim_across = call_sum(mine, arrived)
    to_partner = lax.ppermute(rim_partner, "space", partner)
    to_across = lax.ppermute(rim_across, "space", across)
    total = total.reshape(-1, 16, 128)[:108].astype(F32).reshape(27, out, 128)
    weight_grad = jnp.transpose(total * lax.rsqrt(F32(space * blocks * 512)), (1, 0, 2))

    input_grad = call_final(spot, own, to_partner, to_across, occupancy)
    return (activation, input_grad, weight_grad)


def solution(mesh):
    placed = (
        P("space", "chan", None),
        P("space", None),
        P("chan", None, None),
        P("space", "chan", None),
        P("space", None),
    )
    return jax.shard_map(
        on_device,
        mesh=mesh,
        in_specs=placed,
        out_specs=(P("space", "chan", None), P("space", "chan", None), P("chan", None, None)),
        check_vma=False,
    )
```

```python
import functools

import jax
import jax.numpy as jnp
from jax import lax
from jax.experimental import pallas as pl
from jax.experimental.pallas import tpu as pltpu
from jax.sharding import PartitionSpec as P

F32 = jnp.float32
BF16 = jnp.bfloat16
OFFSETS = [(a, b, c) for a in (-1, 0, 1) for b in (-1, 0, 1) for c in (-1, 0, 1)]
NT = (((1,), (1,)), ((), ()))
CUBE = 1616
WIDE = 640
FLIPS = (2, 1, 3)
VMEM = pl.BlockSpec(memory_space=pltpu.VMEM)
SMEM = pl.BlockSpec(memory_space=pltpu.SMEM)
PARAMS = pltpu.CompilerParams(vmem_limit_bytes=24 * 1024 * 1024)
SMALL = pltpu.CompilerParams(vmem_limit_bytes=8 * 1024 * 1024)


def spans(shift):
    if shift < 0:
        return [(0, 7)]
    if shift > 0:
        return [(9, 0)]
    return [(1 + i, i) for i in range(8)]


def slot_of(spot, listed, block, number, blocks):
    if number == 13:
        return block
    name = listed[block, number if number < 13 else number - 1]
    local = name - spot[0] * blocks
    is_even = lax.rem(spot[0], 2) == 0
    below = jnp.where(is_even, blocks + 1, blocks)
    above = jnp.where(is_even, blocks, blocks + 1)
    local = jnp.where(local == -1, below, jnp.where(local == blocks, above, local))
    return jnp.where(name < 0, blocks + 2, local)


def fill_cube(spot, listed, block, blocks, voxels, cube, base):
    for number, (a, b, c) in enumerate(OFFSETS):
        first = pl.multiple_of(slot_of(spot, listed, block, number, blocks) * 512, 512)
        for i_to, i_from in spans(a):
            if c == 0:
                for j_to, j_from in spans(b):
                    row = base + (i_to * 10 + j_to) * 16 + 8
                    cube[row : row + 8, :] = voxels[pl.ds(first + i_from * 64 + j_from * 8, 8), :]
                continue
            k_from, k_to = (7, 7) if c < 0 else (0, 16)
            if b == 0:
                source = pl.ds(first + i_from * 64 + k_from, 8, stride=8)
                cube[pl.ds(base + (i_to * 10 + 1) * 16 + k_to, 8, stride=16), :] = voxels[source, :]
            else:
                ((j_to, j_from),) = spans(b)
                row = base + (i_to * 10 + j_to) * 16 + k_to
                source = pl.ds(first + i_from * 64 + j_from * 8 + k_from, 1)
                cube[row : row + 1, :] = voxels[source, :]


def pack_patches(cube, base, patches, top):
    for i in range(10):
        for c in range(3):
            rows = [
                cube[base + (i * 10 + j) * 16 + 7 + c : base + (i * 10 + j) * 16 + 15 + c, :]
                for j in range(10)
            ]
            pairs = [
                jnp.concatenate([rows[j], rows[j + 1]], axis=0).astype(BF16) for j in range(9)
            ]
            for b in range(3):
                lanes = (3 * b + c) * 128
                for t in range(4):
                    row = top + i * 64 + t * 16
                    patches[row : row + 16, lanes : lanes + 128] = pairs[2 * t + b]


def load_block(gathered, occupancy, slot):
    block = jnp.concatenate([gathered[c, slot] for c in range(gathered.shape[0])], axis=0)
    return block.astype(F32) * occupancy[slot : slot + 1, :].astype(F32)


def rim_kernel(spot, gathered, occupancy, to_partner, to_across):
    first = load_block(gathered, occupancy, 0).astype(BF16)
    last = load_block(gathered, occupancy, gathered.shape[1] - 1).astype(BF16)
    is_even = lax.rem(spot[0], 2) == 0
    to_partner[...] = jnp.where(is_even, last, first)
    to_across[...] = jnp.where(is_even, first, last)


def forward_block(
    spot, listed, block, stacked, cotangent, occupancy, voxels, cube, patches, grads, place
):
    base, top = place * CUBE, place * WIDE
    fill_cube(spot, listed, block, cotangent.shape[0], voxels, cube, base)
    pack_patches(cube, base, patches, top)
    wide = lax.dot_general(
        stacked[...], patches[top : top + WIDE, :], NT, preferred_element_type=F32
    )
    pre = (
        wide[0:64, 0:512]
        + pltpu.roll(wide[64:128], WIDE - 64, 1)[:, 0:512]
        + wide[128:192, 128:640]
    )
    live = occupancy[block : block + 1, :].astype(F32)
    sigma = jax.nn.sigmoid(pre)
    slope = sigma * (1.0 + pre * (1.0 - sigma))
    grad = (cotangent[block].astype(F32) * slope * live).astype(BF16).astype(F32)
    grad = jnp.concatenate([grad, jnp.zeros((64, 128), F32)], axis=1)
    lanes = slice(top, top + WIDE)
    grads[0:64, lanes] = grad.astype(BF16)
    grads[64:128, lanes] = pltpu.roll(grad, 64, 1).astype(BF16)
    grads[128:192, lanes] = pltpu.roll(grad, 128, 1).astype(BF16)
    return (pre * sigma * live).astype(BF16)


def own_voxels(gathered, occupancy, voxels):
    blocks = gathered.shape[1]
    for slot in range(blocks):
        block = load_block(gathered, occupancy, slot)
        voxels[slot * 512 : (slot + 1) * 512, :] = block.T
    voxels[(blocks + 2) * 512 : (blocks + 3) * 512, :] = jnp.zeros((512, 128), F32)


def inner_kernel(
    spot, listed, gathered, weight, cotangent, occupancy,
    activation, stacked, grads, product, own,
    voxels, cube, patches,
):
    blocks = cotangent.shape[0]
    out = weight.shape[1]
    for number in range(27):
        a, lanes = number // 9, number % 9 * 128
        stacked[a * out : (a + 1) * out, lanes : lanes + 128] = weight[number]
    own_voxels(gathered, occupancy, voxels)
    own[...] = voxels[0 : blocks * 512, :]
    for block in range(1, blocks - 1):
        activation[block - 1] = forward_block(
            spot, listed, block, stacked, cotangent, occupancy, voxels, cube, patches, grads,
            block - 1,
        )
    for first in range(0, 9, 2):
        lanes = slice(first * 128, min(first + 2, 9) * 128)
        product[:, lanes] = jnp.dot(grads[...], patches[:, lanes], preferred_element_type=F32)


def outer_kernel(
    spot, listed, own, from_across, from_partner, cotangent, occupancy, inner, stacked, product,
    activation, grads, tiles,
    voxels, cube, patches,
):
    blocks = cotangent.shape[0]
    voxels[0 : blocks * 512, :] = own[...]
    voxels[(blocks + 2) * 512 : (blocks + 3) * 512, :] = jnp.zeros((512, 128), F32)
    for slot, rim in ((blocks, from_partner), (blocks + 1, from_across)):
        voxels[slot * 512 : (slot + 1) * 512, :] = rim[...].astype(F32).T
    activation[1 : blocks - 1] = inner[...]
    for place, block in enumerate((0, blocks - 1)):
        activation[block] = forward_block(
            spot, listed, block, stacked, cotangent, occupancy, voxels, cube, patches, grads, place
        )
    for first in range(0, 9, 2):
        count = min(2, 9 - first)
        lanes = slice(first * 128, (first + count) * 128)
        part = product[:, lanes] + jnp.dot(
            grads[...], patches[:, lanes], preferred_element_type=F32
        )
        for t in range(count):
            for r in range(12):
                corner = part[r * 16 : (r + 1) * 16, t * 128 : (t + 1) * 128]
                tiles[(r // 4 * 9 + first + t) * 4 + r % 4] = corner.astype(BF16)
    for t in range(108, tiles.shape[0]):
        tiles[t] = jnp.zeros((16, 128), BF16)


def add_gradients(spot, listed, picked, blocks, stacked, grads, sums, wide):
    edge = lax.broadcasted_iota(jnp.int32, (8, 128), 0)
    for at, p in enumerate(picked):
        turn = grads[:, at * WIDE : (at + 1) * WIDE].astype(F32).T.astype(BF16)
        wide[...] = jnp.dot(turn, stacked[...], preferred_element_type=F32)
        for i in range(10):
            a, i_to = (-1, 7) if i == 0 else ((1, 0) if i == 9 else (0, i - 1))

            def line(j, c):
                total = None
                for b in range(3):
                    if 0 <= j - b < 8:
                        row = i * 64 + (j - b) * 8
                        lanes = (3 * b + c) * 128
                        term = wide[row : row + 8, lanes : lanes + 128]
                        total = term if total is None else total + term
                return total

            for b, js in ((-1, [0]), (0, list(range(1, 9))), (1, [9])):
                before = [pltpu.roll(line(j, 0), 7, 0) for j in js]
                centre = [line(j, 1) for j in js]
                after = [pltpu.roll(line(j, 2), 1, 0) for j in js]
                j_to = 7 if b < 0 else 0
                for c in (-1, 0, 1):
                    if c < 0:
                        parts = [jnp.where(edge == 7, x, 0.0) for x in before]
                    elif c > 0:
                        parts = [jnp.where(edge == 0, x, 0.0) for x in after]
                    else:
                        parts = [
                            y + jnp.where(edge < 7, x, 0.0) + jnp.where(edge > 0, z, 0.0)
                            for x, y, z in zip(before, centre, after)
                        ]
                    part = parts[0] if len(parts) == 1 else jnp.concatenate(parts, axis=0)
                    number = 9 * (a + 1) + 3 * (b + 1) + c + 1
                    slot = slot_of(spot, listed, p, number, blocks)
                    first = pl.multiple_of(slot * 512, 512)
                    rows = pl.ds(first + i_to * 64 + j_to * 8, 8 * len(js))
                    sums[rows, :] = sums[rows, :] + part


def backward_kernel(
    blocks, spot, ring_spot, listed, stacked, inner, outer, mine, *rest
):
    sends, (sums, wide, turned) = rest[:-3], rest[-3:]
    sums[...] = jnp.zeros_like(sums)
    add_gradients(spot, listed, (0, blocks - 1), blocks, stacked, outer, sums, wide)
    add_gradients(spot, listed, range(1, blocks - 1), blocks, stacked, inner, sums, wide)
    share = mine.shape[1]
    for slot in range(blocks + 2):
        turned[slot * 128 : (slot + 1) * 128, :] = sums[slot * 512 : (slot + 1) * 512, :].T
    for flip, ref in zip((0,) + FLIPS, (mine,) + tuple(sends)):
        row = pl.multiple_of((ring_spot[0] ^ flip) * share, share)
        for slot in range(blocks + 2):
            ref[slot] = turned[pl.ds(slot * 128 + row, share), :].astype(ref.dtype)


def shape(*dims, dtype=BF16):
    return jax.ShapeDtypeStruct(dims, dtype)


def call_rims(spot, gathered, occupancy):
    rim = shape(128, 512)
    return pl.pallas_call(
        rim_kernel,
        out_shape=[rim, rim],
        in_specs=[SMEM, VMEM, VMEM],
        out_specs=[VMEM] * 2,
        compiler_params=SMALL,
        cost_estimate=pl.CostEstimate(flops=10**6, bytes_accessed=10**6, transcendentals=0),
    )(spot, gathered, occupancy)


def scratch_of(blocks, count):
    return [
        pltpu.VMEM(((blocks + 3) * 512, 128), F32),
        pltpu.VMEM((count * CUBE, 128), F32),
        pltpu.VMEM((count * WIDE, 1152), BF16),
    ]


def call_inner(spot, listed, gathered, weight, cotangent, occupancy):
    blocks, out = cotangent.shape[:2]
    return pl.pallas_call(
        inner_kernel,
        out_shape=[
            shape(blocks - 2, out, 512),
            shape(3 * out, 1152),
            shape(3 * out, (blocks - 2) * WIDE),
            shape(3 * out, 1152, dtype=F32),
            shape(blocks * 512, 128, dtype=F32),
        ],
        in_specs=[SMEM] * 2 + [VMEM] * 4,
        out_specs=[VMEM] * 5,
        scratch_shapes=scratch_of(blocks, blocks - 2),
        compiler_params=PARAMS,
        cost_estimate=pl.CostEstimate(flops=10**9, bytes_accessed=4 * 10**6, transcendentals=10**5),
    )(spot, listed, gathered, weight, cotangent, occupancy)


def call_outer(spot, listed, own, rims, cotangent, occupancy, inner, stacked, product, tiles):
    blocks, out = cotangent.shape[:2]
    return pl.pallas_call(
        outer_kernel,
        out_shape=[
            shape(blocks, out, 512),
            shape(3 * out, 2 * WIDE),
            shape(tiles, 16, 128),
        ],
        in_specs=[SMEM] * 2 + [VMEM] * 8,
        out_specs=[VMEM] * 3,
        scratch_shapes=scratch_of(blocks, 2),
        compiler_params=PARAMS,
        cost_estimate=pl.CostEstimate(flops=10**9, bytes_accessed=4 * 10**6, transcendentals=10**5),
    )(spot, listed, own, *rims, cotangent, occupancy, inner, stacked, product)


def call_backward(spot, ring_spot, listed, stacked, inner, outer, chan):
    blocks = listed.shape[0]
    piece = (blocks + 2, 128 // chan, 512)
    return pl.pallas_call(
        functools.partial(backward_kernel, blocks),
        out_shape=[shape(*piece, dtype=F32)] + [shape(*piece)] * (chan - 1),
        in_specs=[SMEM] * 3 + [VMEM] * 3,
        out_specs=[VMEM] * chan,
        scratch_shapes=[
            pltpu.VMEM(((blocks + 3) * 512, 128), F32),
            pltpu.VMEM((WIDE, 1152), F32),
            pltpu.VMEM(((blocks + 2) * 128, 512), F32),
        ],
        compiler_params=PARAMS,
        cost_estimate=pl.CostEstimate(flops=2 * 10**9, bytes_accessed=8 * 10**6, transcendentals=0),
    )(spot, ring_spot, listed, stacked, inner, outer)


def add_kernel(copies, pieces, out):
    total = pieces[0].astype(F32)
    for n in range(1, pieces.shape[0]):
        total = total + pieces[n].astype(F32)
    for n in range(copies):
        out[n] = total.astype(BF16)


def call_add(pieces, copies):
    return pl.pallas_call(
        functools.partial(add_kernel, copies),
        out_shape=shape(copies, *pieces.shape[1:]),
        in_specs=[VMEM],
        out_specs=VMEM,
        compiler_params=SMALL,
    )(pieces)


def sum_kernel(blocks, mine, *refs):
    arrived, (own, to_partner, to_across) = refs[:-3], refs[-3:]
    for slot in range(blocks + 2):
        total = mine[slot]
        for ref in arrived:
            total = total + ref[slot].astype(F32)
        if slot < blocks:
            own[slot] = total
        else:
            (to_partner if slot == blocks else to_across)[...] = total.astype(BF16)


def call_sum(mine, arrived):
    blocks, rim = mine.shape[0] - 2, mine.shape[1:]
    return pl.pallas_call(
        functools.partial(sum_kernel, blocks),
        out_shape=[shape(blocks, *rim, dtype=F32), shape(*rim), shape(*rim)],
        in_specs=[VMEM] * (1 + len(arrived)),
        out_specs=[VMEM] * 3,
        compiler_params=SMALL,
    )(mine, *arrived)


def final_kernel(spot, own, from_across, from_partner, occupancy, out):
    blocks = own.shape[0]
    is_even = lax.rem(spot[0], 2) == 0
    partner, across = from_partner[...].astype(F32), from_across[...].astype(F32)
    for slot in range(blocks):
        total = own[slot]
        if slot == 0:
            total = total + jnp.where(is_even, across, partner)
        if slot == blocks - 1:
            total = total + jnp.where(is_even, partner, across)
        out[slot] = (total * occupancy[slot : slot + 1, :].astype(F32)).astype(BF16)


def call_final(spot, own, from_across, from_partner, occupancy):
    return pl.pallas_call(
        final_kernel,
        out_shape=shape(*own.shape),
        in_specs=[SMEM] + [VMEM] * 4,
        out_specs=VMEM,
        compiler_params=SMALL,
    )(spot, own, from_across, from_partner, occupancy)


def stages_of(count):
    return {128: (4, 16, 2), 4: (2, 1, 2), 8: (2, 2, 2), 16: (2, 4, 2)}[count]


def exchange(pieces, groups):
    return lax.all_to_all(pieces, "space", 0, 0, axis_index_groups=groups)


def groups_of(space):
    columns, rows, cores = stages_of(space)
    near, far = {}, {}
    for index in range(space):
        y, z, core = index // (rows * cores), index // cores % rows, index % cores
        near.setdefault(z // 2, []).append(index)
        far.setdefault((y, core, z % 2), []).append(index)
    return list(near.values()), list(far.values())


def on_device(features, occupancy, weight, cotangent, neighbours):
    blocks = features.shape[0]
    out = weight.shape[0]
    space = lax.axis_size("space")
    chan = lax.axis_size("chan")
    near, far = groups_of(space)
    share = -(-108 // len(near[0]))
    place = lax.axis_index("space")

    partner = [(i, i ^ 1) for i in range(space)]
    across = [(i, i - 1 if i % 2 == 0 else i + 1) for i in range(1, space - 1)]
    spot = place.astype(jnp.int32).reshape(1)
    ring_spot = lax.axis_index("chan").astype(jnp.int32).reshape(1)
    gathered = lax.all_gather(features, "chan", axis=0)
    rim_partner, rim_across = call_rims(spot, gathered, occupancy)
    from_across = lax.ppermute(rim_across, "space", across)
    from_partner = lax.ppermute(rim_partner, "space", partner)
    rims = (from_across, from_partner)

    inner, stacked, inner_grads, product, own = call_inner(
        spot, neighbours, gathered, jnp.transpose(weight, (1, 0, 2)), cotangent, occupancy
    )
    activation, outer_grads, tiles = call_outer(
        spot, neighbours, own, rims, cotangent, occupancy, inner, stacked, product,
        len(near[0]) * share,
    )

    parts = exchange(tiles.reshape(len(near[0]), share, 16, 128), near)
    mine, *sends = call_backward(
        spot, ring_spot, neighbours, stacked, inner_grads, outer_grads, chan
    )
    parts, mine, sends = lax.optimization_barrier((parts, mine, sends))
    parts = exchange(call_add(parts, len(far[0])), far)
    arrived = [
        lax.ppermute(piece, "chan", [(c, c ^ flip) for c in range(chan)])
        for flip, piece in zip(FLIPS, sends)
    ]
    parts, arrived = lax.optimization_barrier((parts, arrived))
    total = exchange(call_add(parts, len(near[0])), near)
    own, rim_partner, rim_across = call_sum(mine, arrived)
    to_across = lax.ppermute(rim_across, "space", across)
    to_partner = lax.ppermute(rim_partner, "space", partner)
    total = total.reshape(-1, 16, 128)[:108].astype(F32).reshape(27, out, 128)
    weight_grad = jnp.transpose(total * lax.rsqrt(F32(space * blocks * 512)), (1, 0, 2))

    input_grad = call_final(spot, own, to_across, to_partner, occupancy)
    return (activation, input_grad, weight_grad)


def solution(mesh):
    placed = (
        P("space", "chan", None),
        P("space", None),
        P("chan", None, None),
        P("space", "chan", None),
        P("space", None),
    )
    return jax.shard_map(
        on_device,
        mesh=mesh,
        in_specs=placed,
        out_specs=(P("space", "chan", None), P("space", "chan", None), P("chan", None, None)),
        check_vma=False,
    )
```

```python
import functools

import jax
import jax.numpy as jnp
from jax import lax
from jax.experimental import pallas as pl
from jax.experimental.pallas import tpu as pltpu
from jax.sharding import PartitionSpec as P

F32 = jnp.float32
BF16 = jnp.bfloat16
OFFSETS = [(a, b, c) for a in (-1, 0, 1) for b in (-1, 0, 1) for c in (-1, 0, 1)]
NT = (((1,), (1,)), ((), ()))
CUBE = 1616
WIDE = 640
FLIPS = (2, 1, 3)
VMEM = pl.BlockSpec(memory_space=pltpu.VMEM)
SMEM = pl.BlockSpec(memory_space=pltpu.SMEM)
HBM = pl.BlockSpec(memory_space=pltpu.HBM)
PARAMS = pltpu.CompilerParams(vmem_limit_bytes=24 * 1024 * 1024)
SMALL = pltpu.CompilerParams(vmem_limit_bytes=8 * 1024 * 1024)


def spans(shift):
    if shift < 0:
        return [(0, 7)]
    if shift > 0:
        return [(9, 0)]
    return [(1 + i, i) for i in range(8)]


def slot_of(spot, listed, block, number, blocks):
    if number == 13:
        return block
    name = listed[block, number if number < 13 else number - 1]
    local = name - spot[0] * blocks
    is_even = lax.rem(spot[0], 2) == 0
    below = jnp.where(is_even, blocks + 1, blocks)
    above = jnp.where(is_even, blocks, blocks + 1)
    local = jnp.where(local == -1, below, jnp.where(local == blocks, above, local))
    return jnp.where(name < 0, blocks + 2, local)


def fill_cube(spot, listed, block, blocks, voxels, cube, base):
    for number, (a, b, c) in enumerate(OFFSETS):
        first = pl.multiple_of(slot_of(spot, listed, block, number, blocks) * 512, 512)
        for i_to, i_from in spans(a):
            if c == 0:
                for j_to, j_from in spans(b):
                    row = base + (i_to * 10 + j_to) * 16 + 8
                    cube[row : row + 8, :] = voxels[pl.ds(first + i_from * 64 + j_from * 8, 8), :]
                continue
            k_from, k_to = (7, 7) if c < 0 else (0, 16)
            if b == 0:
                source = pl.ds(first + i_from * 64 + k_from, 8, stride=8)
                cube[pl.ds(base + (i_to * 10 + 1) * 16 + k_to, 8, stride=16), :] = voxels[source, :]
            else:
                ((j_to, j_from),) = spans(b)
                row = base + (i_to * 10 + j_to) * 16 + k_to
                source = pl.ds(first + i_from * 64 + j_from * 8 + k_from, 1)
                cube[row : row + 1, :] = voxels[source, :]


def pack_patches(cube, base, patches, top):
    for i in range(10):
        for c in range(3):
            rows = [
                cube[base + (i * 10 + j) * 16 + 7 + c : base + (i * 10 + j) * 16 + 15 + c, :]
                for j in range(10)
            ]
            pairs = [
                jnp.concatenate([rows[j], rows[j + 1]], axis=0).astype(BF16) for j in range(9)
            ]
            for b in range(3):
                lanes = (3 * b + c) * 128
                for t in range(4):
                    row = top + i * 64 + t * 16
                    patches[row : row + 16, lanes : lanes + 128] = pairs[2 * t + b]


def load_block(gathered, occupancy, slot):
    block = jnp.concatenate([gathered[c, slot] for c in range(gathered.shape[0])], axis=0)
    return block.astype(F32) * occupancy[slot : slot + 1, :].astype(F32)


def rim_kernel(spot, gathered, occupancy, to_partner, to_across):
    first = load_block(gathered, occupancy, 0).astype(BF16)
    last = load_block(gathered, occupancy, gathered.shape[1] - 1).astype(BF16)
    is_even = lax.rem(spot[0], 2) == 0
    to_partner[...] = jnp.where(is_even, last, first)
    to_across[...] = jnp.where(is_even, first, last)


def forward_block(
    spot, listed, block, stacked, cotangent, occupancy, voxels, cube, patches, grads, place
):
    base, top = place * CUBE, place * WIDE
    fill_cube(spot, listed, block, cotangent.shape[0], voxels, cube, base)
    pack_patches(cube, base, patches, top)
    wide = lax.dot_general(
        stacked[...], patches[top : top + WIDE, :], NT, preferred_element_type=F32
    )
    pre = (
        wide[0:64, 0:512]
        + pltpu.roll(wide[64:128], WIDE - 64, 1)[:, 0:512]
        + wide[128:192, 128:640]
    )
    live = occupancy[block : block + 1, :].astype(F32)
    sigma = jax.nn.sigmoid(pre)
    slope = sigma * (1.0 + pre * (1.0 - sigma))
    grad = (cotangent[block].astype(F32) * slope * live).astype(BF16).astype(F32)
    grad = jnp.concatenate([grad, jnp.zeros((64, 128), F32)], axis=1)
    lanes = slice(top, top + WIDE)
    grads[0:64, lanes] = grad.astype(BF16)
    grads[64:128, lanes] = pltpu.roll(grad, 64, 1).astype(BF16)
    grads[128:192, lanes] = pltpu.roll(grad, 128, 1).astype(BF16)
    return (pre * sigma * live).astype(BF16)


def own_voxels(gathered, occupancy, voxels):
    blocks = gathered.shape[1]
    for slot in range(blocks):
        block = load_block(gathered, occupancy, slot)
        voxels[slot * 512 : (slot + 1) * 512, :] = block.T
    voxels[(blocks + 2) * 512 : (blocks + 3) * 512, :] = jnp.zeros((512, 128), F32)


def inner_kernel(
    spot, listed, gathered, weight, cotangent, occupancy,
    activation, stacked, grads, product, own,
    voxels, cube, patches,
):
    blocks = cotangent.shape[0]
    out = weight.shape[1]
    for number in range(27):
        a, lanes = number // 9, number % 9 * 128
        stacked[a * out : (a + 1) * out, lanes : lanes + 128] = weight[number]
    own_voxels(gathered, occupancy, voxels)
    own[...] = voxels[0 : blocks * 512, :]
    for block in range(1, blocks - 1):
        activation[block - 1] = forward_block(
            spot, listed, block, stacked, cotangent, occupancy, voxels, cube, patches, grads,
            block - 1,
        )
    for first in range(0, 9, 2):
        lanes = slice(first * 128, min(first + 2, 9) * 128)
        product[:, lanes] = jnp.dot(grads[...], patches[:, lanes], preferred_element_type=F32)


def outer_kernel(
    spot, listed, own, from_across, from_partner, cotangent, occupancy, inner, stacked, product,
    activation_hbm, grads, tiles_hbm,
    voxels, cube, patches, activation, tiles, semaphores,
):
    blocks = cotangent.shape[0]
    voxels[0 : blocks * 512, :] = own[...]
    voxels[(blocks + 2) * 512 : (blocks + 3) * 512, :] = jnp.zeros((512, 128), F32)
    for slot, rim in ((blocks, from_partner), (blocks + 1, from_across)):
        voxels[slot * 512 : (slot + 1) * 512, :] = rim[...].astype(F32).T
    activation[1 : blocks - 1] = inner[...]
    for place, block in enumerate((0, blocks - 1)):
        activation[block] = forward_block(
            spot, listed, block, stacked, cotangent, occupancy, voxels, cube, patches, grads, place
        )
    copies = [pltpu.make_async_copy(activation, activation_hbm, semaphores.at[0])]
    copies[0].start()

    def send(first, count):
        rows = pl.ds(first, count)
        copy = pltpu.make_async_copy(
            tiles.at[rows], tiles_hbm.at[rows], semaphores.at[len(copies)]
        )
        copy.start()
        copies.append(copy)

    if tiles.shape[0] > 108:
        for t in range(108, tiles.shape[0]):
            tiles[t] = jnp.zeros((16, 128), BF16)
        send(108, tiles.shape[0] - 108)
    for first in range(0, 9, 2):
        count = min(2, 9 - first)
        lanes = slice(first * 128, (first + count) * 128)
        part = product[:, lanes] + jnp.dot(
            grads[...], patches[:, lanes], preferred_element_type=F32
        )
        for t in range(count):
            for r in range(12):
                corner = part[r * 16 : (r + 1) * 16, t * 128 : (t + 1) * 128]
                tiles[(r // 4 * 9 + first + t) * 4 + r % 4] = corner.astype(BF16)
        for a in range(3):
            send((a * 9 + first) * 4, count * 4)
    for copy in copies:
        copy.wait()


def add_gradients(spot, listed, picked, blocks, stacked, grads, sums, wide):
    edge = lax.broadcasted_iota(jnp.int32, (8, 128), 0)
    for at, p in enumerate(picked):
        turn = grads[:, at * WIDE : (at + 1) * WIDE].astype(F32).T.astype(BF16)
        wide[...] = jnp.dot(turn, stacked[...], preferred_element_type=F32)
        for i in range(10):
            a, i_to = (-1, 7) if i == 0 else ((1, 0) if i == 9 else (0, i - 1))

            def line(j, c):
                total = None
                for b in range(3):
                    if 0 <= j - b < 8:
                        row = i * 64 + (j - b) * 8
                        lanes = (3 * b + c) * 128
                        term = wide[row : row + 8, lanes : lanes + 128]
                        total = term if total is None else total + term
                return total

            for b, js in ((-1, [0]), (0, list(range(1, 9))), (1, [9])):
                before = [pltpu.roll(line(j, 0), 7, 0) for j in js]
                centre = [line(j, 1) for j in js]
                after = [pltpu.roll(line(j, 2), 1, 0) for j in js]
                j_to = 7 if b < 0 else 0
                for c in (-1, 0, 1):
                    if c < 0:
                        parts = [jnp.where(edge == 7, x, 0.0) for x in before]
                    elif c > 0:
                        parts = [jnp.where(edge == 0, x, 0.0) for x in after]
                    else:
                        parts = [
                            y + jnp.where(edge < 7, x, 0.0) + jnp.where(edge > 0, z, 0.0)
                            for x, y, z in zip(before, centre, after)
                        ]
                    part = parts[0] if len(parts) == 1 else jnp.concatenate(parts, axis=0)
                    number = 9 * (a + 1) + 3 * (b + 1) + c + 1
                    slot = slot_of(spot, listed, p, number, blocks)
                    first = pl.multiple_of(slot * 512, 512)
                    rows = pl.ds(first + i_to * 64 + j_to * 8, 8 * len(js))
                    sums[rows, :] = sums[rows, :] + part


def backward_kernel(
    blocks, spot, ring_spot, listed, stacked, inner, outer, mine, *rest
):
    sends, (sums, wide, turned) = rest[:-3], rest[-3:]
    sums[...] = jnp.zeros_like(sums)
    add_gradients(spot, listed, (0, blocks - 1), blocks, stacked, outer, sums, wide)
    add_gradients(spot, listed, range(1, blocks - 1), blocks, stacked, inner, sums, wide)
    share = mine.shape[1]
    for slot in range(blocks + 2):
        turned[slot * 128 : (slot + 1) * 128, :] = sums[slot * 512 : (slot + 1) * 512, :].T
    for flip, ref in zip((0,) + FLIPS, (mine,) + tuple(sends)):
        row = pl.multiple_of((ring_spot[0] ^ flip) * share, share)
        for slot in range(blocks + 2):
            ref[slot] = turned[pl.ds(slot * 128 + row, share), :].astype(ref.dtype)


def shape(*dims, dtype=BF16):
    return jax.ShapeDtypeStruct(dims, dtype)


def call_rims(spot, gathered, occupancy):
    rim = shape(128, 512)
    return pl.pallas_call(
        rim_kernel,
        out_shape=[rim, rim],
        in_specs=[SMEM, VMEM, VMEM],
        out_specs=[VMEM] * 2,
        compiler_params=SMALL,
        cost_estimate=pl.CostEstimate(flops=10**6, bytes_accessed=10**6, transcendentals=0),
    )(spot, gathered, occupancy)


def scratch_of(blocks, count):
    return [
        pltpu.VMEM(((blocks + 3) * 512, 128), F32),
        pltpu.VMEM((count * CUBE, 128), F32),
        pltpu.VMEM((count * WIDE, 1152), BF16),
    ]


def call_inner(spot, listed, gathered, weight, cotangent, occupancy):
    blocks, out = cotangent.shape[:2]
    return pl.pallas_call(
        inner_kernel,
        out_shape=[
            shape(blocks - 2, out, 512),
            shape(3 * out, 1152),
            shape(3 * out, (blocks - 2) * WIDE),
            shape(3 * out, 1152, dtype=F32),
            shape(blocks * 512, 128, dtype=F32),
        ],
        in_specs=[SMEM] * 2 + [VMEM] * 4,
        out_specs=[VMEM] * 5,
        scratch_shapes=scratch_of(blocks, blocks - 2),
        compiler_params=PARAMS,
        cost_estimate=pl.CostEstimate(flops=10**9, bytes_accessed=4 * 10**6, transcendentals=10**5),
    )(spot, listed, gathered, weight, cotangent, occupancy)


def call_outer(spot, listed, own, rims, cotangent, occupancy, inner, stacked, product, tiles):
    blocks, out = cotangent.shape[:2]
    return pl.pallas_call(
        outer_kernel,
        out_shape=[
            shape(blocks, out, 512),
            shape(3 * out, 2 * WIDE),
            shape(tiles, 16, 128),
        ],
        in_specs=[SMEM] * 2 + [VMEM] * 8,
        out_specs=[HBM, VMEM, HBM],
        scratch_shapes=scratch_of(blocks, 2)
        + [
            pltpu.VMEM((blocks, out, 512), BF16),
            pltpu.VMEM((tiles, 16, 128), BF16),
            pltpu.SemaphoreType.DMA((17,)),
        ],
        compiler_params=PARAMS,
        cost_estimate=pl.CostEstimate(flops=10**9, bytes_accessed=4 * 10**6, transcendentals=10**5),
    )(spot, listed, own, *rims, cotangent, occupancy, inner, stacked, product)


def call_backward(spot, ring_spot, listed, stacked, inner, outer, chan):
    blocks = listed.shape[0]
    piece = (blocks + 2, 128 // chan, 512)
    return pl.pallas_call(
        functools.partial(backward_kernel, blocks),
        out_shape=[shape(*piece, dtype=F32)] + [shape(*piece)] * (chan - 1),
        in_specs=[SMEM] * 3 + [VMEM] * 3,
        out_specs=[VMEM] * chan,
        scratch_shapes=[
            pltpu.VMEM(((blocks + 3) * 512, 128), F32),
            pltpu.VMEM((WIDE, 1152), F32),
            pltpu.VMEM(((blocks + 2) * 128, 512), F32),
        ],
        compiler_params=PARAMS,
        cost_estimate=pl.CostEstimate(flops=2 * 10**9, bytes_accessed=8 * 10**6, transcendentals=0),
    )(spot, ring_spot, listed, stacked, inner, outer)


def add_kernel(copies, pieces, out):
    total = pieces[0].astype(F32)
    for n in range(1, pieces.shape[0]):
        total = total + pieces[n].astype(F32)
    for n in range(copies):
        out[n] = total.astype(BF16)


def call_add(pieces, copies):
    return pl.pallas_call(
        functools.partial(add_kernel, copies),
        out_shape=shape(copies, *pieces.shape[1:]),
        in_specs=[VMEM],
        out_specs=VMEM,
        compiler_params=SMALL,
    )(pieces)


def sum_kernel(blocks, mine, *refs):
    arrived, (own, to_partner, to_across) = refs[:-3], refs[-3:]
    for slot in range(blocks + 2):
        total = mine[slot]
        for ref in arrived:
            total = total + ref[slot].astype(F32)
        if slot < blocks:
            own[slot] = total
        else:
            (to_partner if slot == blocks else to_across)[...] = total.astype(BF16)


def call_sum(mine, arrived):
    blocks, rim = mine.shape[0] - 2, mine.shape[1:]
    return pl.pallas_call(
        functools.partial(sum_kernel, blocks),
        out_shape=[shape(blocks, *rim, dtype=F32), shape(*rim), shape(*rim)],
        in_specs=[VMEM] * (1 + len(arrived)),
        out_specs=[VMEM] * 3,
        compiler_params=SMALL,
    )(mine, *arrived)


def final_kernel(spot, own, from_across, from_partner, occupancy, out):
    blocks = own.shape[0]
    is_even = lax.rem(spot[0], 2) == 0
    partner, across = from_partner[...].astype(F32), from_across[...].astype(F32)
    for slot in range(blocks):
        total = own[slot]
        if slot == 0:
            total = total + jnp.where(is_even, across, partner)
        if slot == blocks - 1:
            total = total + jnp.where(is_even, partner, across)
        out[slot] = (total * occupancy[slot : slot + 1, :].astype(F32)).astype(BF16)


def call_final(spot, own, from_across, from_partner, occupancy):
    return pl.pallas_call(
        final_kernel,
        out_shape=shape(*own.shape),
        in_specs=[SMEM] + [VMEM] * 4,
        out_specs=VMEM,
        compiler_params=SMALL,
    )(spot, own, from_across, from_partner, occupancy)


def stages_of(count):
    return {128: (4, 16, 2), 4: (2, 1, 2), 8: (2, 2, 2), 16: (2, 4, 2)}[count]


def exchange(pieces, groups):
    return lax.all_to_all(pieces, "space", 0, 0, axis_index_groups=groups)


def groups_of(space):
    columns, rows, cores = stages_of(space)
    near, far = {}, {}
    for index in range(space):
        y, z, core = index // (rows * cores), index // cores % rows, index % cores
        near.setdefault(z // 2, []).append(index)
        far.setdefault((y, core, z % 2), []).append(index)
    return list(near.values()), list(far.values())


def on_device(features, occupancy, weight, cotangent, neighbours):
    blocks = features.shape[0]
    out = weight.shape[0]
    space = lax.axis_size("space")
    chan = lax.axis_size("chan")
    near, far = groups_of(space)
    share = -(-108 // len(near[0]))
    place = lax.axis_index("space")

    partner = [(i, i ^ 1) for i in range(space)]
    across = [(i, i - 1 if i % 2 == 0 else i + 1) for i in range(1, space - 1)]
    spot = place.astype(jnp.int32).reshape(1)
    ring_spot = lax.axis_index("chan").astype(jnp.int32).reshape(1)
    gathered = lax.all_gather(features, "chan", axis=0)
    rim_partner, rim_across = call_rims(spot, gathered, occupancy)
    from_across = lax.ppermute(rim_across, "space", across)
    from_partner = lax.ppermute(rim_partner, "space", partner)
    rims = (from_across, from_partner)

    inner, stacked, inner_grads, product, own = call_inner(
        spot, neighbours, gathered, jnp.transpose(weight, (1, 0, 2)), cotangent, occupancy
    )
    activation, outer_grads, tiles = call_outer(
        spot, neighbours, own, rims, cotangent, occupancy, inner, stacked, product,
        len(near[0]) * share,
    )

    parts = exchange(tiles.reshape(len(near[0]), share, 16, 128), near)
    mine, *sends = call_backward(
        spot, ring_spot, neighbours, stacked, inner_grads, outer_grads, chan
    )
    parts, mine, sends = lax.optimization_barrier((parts, mine, sends))
    parts = exchange(call_add(parts, len(far[0])), far)
    arrived = [
        lax.ppermute(piece, "chan", [(c, c ^ flip) for c in range(chan)])
        for flip, piece in zip(FLIPS, sends)
    ]
    parts, arrived = lax.optimization_barrier((parts, arrived))
    total = exchange(call_add(parts, len(near[0])), near)
    own, rim_partner, rim_across = call_sum(mine, arrived)
    to_across = lax.ppermute(rim_across, "space", across)
    to_partner = lax.ppermute(rim_partner, "space", partner)
    total = total.reshape(-1, 16, 128)[:108].astype(F32).reshape(27, out, 128)
    weight_grad = jnp.transpose(total * lax.rsqrt(F32(space * blocks * 512)), (1, 0, 2))

    input_grad = call_final(spot, own, to_across, to_partner, occupancy)
    return (activation, input_grad, weight_grad)


def solution(mesh):
    placed = (
        P("space", "chan", None),
        P("space", None),
        P("chan", None, None),
        P("space", "chan", None),
        P("space", None),
    )
    return jax.shard_map(
        on_device,
        mesh=mesh,
        in_specs=placed,
        out_specs=(P("space", "chan", None), P("space", "chan", None), P("chan", None, None)),
        check_vma=False,
    )
```
